128 devices in a mesh: seq: 32 (over z_lo, y, x), tp: 4 (over z_hi, core).
Axes of the slice: x: 4, y: 4, z: 4 (z_hi: 2, z_lo: 2; z = z_hi * 2 + z_lo), core: 2. Of those that a mesh axis runs over, the one named last changes fastest.
Arguments:
- queries: bfloat16 [8192, 1536], P('seq', 'tp'), may hold values from -6 to 6
- key_rows: bfloat16 [8192, 1536], P('seq', 'tp'), may hold values from -6 to 6
- value_rows: bfloat16 [8192, 1536], P('seq', 'tp'), may hold values from -6 to 6
- residual: bfloat16 [8192, 1536], P('seq'), may hold values from -4 to 4
- branch_gate: float32 [1536], replicated, may hold values from 1 to 4
- out_weight: bfloat16 [1536, 1536], P('tp'), may hold values from -0.15625 to 0.15625
- final_scale: float32 [1536], replicated, may hold values from 0.25 to 1.75
- final_shift: float32 [1536], replicated, may hold values from -3 to 3
- final_weight: bfloat16 [1536, 64], replicated, may hold values from -0.15625 to 0.15625
- input_conv: bfloat16 [7, 64, 2048], replicated, may hold values from -0.25 to 0.25
- lift_slopes: float32 [2048], replicated, may hold values from 0.5 to 2
- up_weight: bfloat16 [2048, 16, 512], P(None, None, 'tp'), may hold values from -0.09375 to 0.09375
- unit_slopes: float32 [3, 2, 512], P(None, None, 'tp'), may hold values from 0.5 to 2
- unit_dilated: bfloat16 [3, 7, 512, 512], P(None, None, None, 'tp'), may hold values from -0.09375 to 0.09375
- unit_point: bfloat16 [3, 512, 512], P(None, None, 'tp'), may hold values from -0.25 to 0.25
Outputs:
- latent: bfloat16 [8192, 64], P('seq')
- decoded: float32 [65536, 512], P('seq', 'tp')
The draws below stay inside these ranges and needn't reach their ends.
All inputs are finite; a program needn't handle non-finite values.
Results may differ from the reference program's by a relative error of at most 0.035.
Values may be sent and summed in bfloat16 or wider, within the bound.
No kernel may reach another device: no remote copies, remote signals or barrier semaphores. Data moves between devices by JAX's collectives and lax.ppermute only.
A program may use at most 192 MiB of HBM per device.

```python
import math
import jax
import jax.numpy as jnp
from jax import lax

D = 1536
H = 24
HD = 64
LAT = 64
CH0 = 2048
C1 = 512
TOKENS = 8192
NT = 65536


def draw_queries(key, part):
    key = jax.random.fold_in(key, 1)
    field = jnp.clip(1.25 * jax.random.normal(key, (TOKENS, D), jnp.float32), -6.0, 6.0)
    return field.astype(jnp.bfloat16)


def draw_key_rows(key, part):
    key = jax.random.fold_in(key, 2)
    field = jnp.clip(1.25 * jax.random.normal(key, (TOKENS, D), jnp.float32), -6.0, 6.0)
    return field.astype(jnp.bfloat16)


def draw_residual(key, part):
    key = jax.random.fold_in(key, 3)
    noise_key, row_key, column_key = jax.random.split(key, 3)
    row_scales = jnp.exp(math.log(10.0) * jax.random.uniform(row_key, (TOKENS, 1), jnp.float32))
    column_scales = jnp.exp(math.log(3.0) * jax.random.uniform(column_key, (1, D), jnp.float32))
    noise = jnp.clip(jax.random.normal(noise_key, (TOKENS, D), jnp.float32), -6.0, 6.0)
    return (0.02 * row_scales * column_scales * noise).astype(jnp.bfloat16)


def block_levels(own_key, dims, pieces, smallest, top_value):
    loudness = 1.0
    for dim, shards_of in pieces:
        heights = jax.random.uniform(jax.random.fold_in(jax.random.fold_in(own_key, 6), dim), (shards_of,), jnp.float32, smallest / len(pieces), top_value / len(pieces))
        loudness = loudness * jnp.repeat(jnp.exp(heights), dims[dim] // shards_of).reshape((-1,) + (1,) * (len(dims) - 1 - dim))
    return loudness


def scatter_about(stream_key, dims, scale, limit, cuts=(), kind=jnp.bfloat16):
    array = scale * jax.random.normal(stream_key, dims, jnp.float32)
    if cuts:
        array = array * block_levels(stream_key, dims, cuts, -0.22, 0.18)
    return jnp.clip(array, -limit, limit).astype(kind)


def setup_inputs(seed: int = 0) -> dict:
    arg_keys = jax.random.split(jax.random.key(seed), 16)
    queries = draw_queries(jax.random.fold_in(arg_keys[15], 71), 0)
    key_rows = draw_key_rows(jax.random.fold_in(arg_keys[15], 71), 0)
    value_rows = scatter_about(arg_keys[2], (TOKENS, D), 1.0, 6.0, ((0, 32), (1, 4)))
    residual = draw_residual(jax.random.fold_in(arg_keys[15], 71), 0)
    branch_gate = jnp.clip(jnp.exp(jax.random.uniform(arg_keys[4], (D,), jnp.float32, math.log(1.0), math.log(4.0))), 1.0, 4.0)
    out_weight = scatter_about(arg_keys[5], (D, D), D ** -0.5, 0.15625, ((0, 4),))
    final_scale = jnp.clip(1.0 + 0.15 * jax.random.normal(arg_keys[6], (D,), jnp.float32), 0.25, 1.75)
    final_shift = scatter_about(arg_keys[7], (D,), 0.5, 3.0, (), jnp.float32)
    final_weight = scatter_about(arg_keys[8], (D, LAT), D ** -0.5, 0.15625)
    input_conv = scatter_about(arg_keys[9], (7, LAT, CH0), (7 * LAT) ** -0.5, 0.25)
    lift_slopes = jnp.clip(jnp.exp(jax.random.uniform(arg_keys[10], (CH0,), jnp.float32, math.log(0.5), math.log(2.0))), 0.5, 2.0)
    up_weight = scatter_about(arg_keys[11], (CH0, 16, C1), (2 * CH0) ** -0.5, 0.09375, ((2, 4),))
    unit_slopes = jnp.clip(jnp.exp(math.log(2.0) - 1.3862944 * jax.random.uniform(arg_keys[12], (3, 2, C1), jnp.float32) ** block_levels(arg_keys[12], (3, 2, C1), ((2, 4),), -0.2, 0.2)), 0.5, 2.0)
    unit_dilated = scatter_about(arg_keys[13], (3, 7, C1, C1), (7 * C1) ** -0.5, 0.09375, ((3, 4),))
    unit_point = scatter_about(arg_keys[14], (3, C1, C1), C1 ** -0.5, 0.25, ((2, 4),))
    return dict(queries=queries, key_rows=key_rows, value_rows=value_rows, residual=residual, branch_gate=branch_gate, out_weight=out_weight, final_scale=final_scale, final_shift=final_shift, final_weight=final_weight, input_conv=input_conv, lift_slopes=lift_slopes, up_weight=up_weight, unit_slopes=unit_slopes, unit_dilated=unit_dilated, unit_point=unit_point)


def snake(signal, slopes):
    return signal + jnp.sin(slopes * signal) ** 2 / slopes

def one_head(inputs):
    query_head, keyset, valueset = inputs
    scores = jnp.dot(query_head, keyset.T, preferred_element_type=jnp.float32) / math.sqrt(HD)
    weights = jnp.exp(scores - lax.optimization_barrier(jnp.max(scores, axis=1, keepdims=True)))
    probabilities = weights.astype(jnp.bfloat16)
    summed = jnp.dot(probabilities, valueset, preferred_element_type=jnp.float32)
    return (summed / lax.optimization_barrier(jnp.sum(weights, axis=1, keepdims=True))).astype(jnp.bfloat16)

def dilated(signal, weight, spread, length):
    summed = jnp.zeros((length, weight.shape[2]), jnp.float32)
    for tap_index in range(weight.shape[0]):
        summed = summed + jnp.dot(signal[tap_index * spread:tap_index * spread + length], weight[tap_index], preferred_element_type=jnp.float32)
    return summed

def upsample(beside_all, weight):
    stride = weight.shape[1] // 2
    half_stride = stride // 2
    weight_float = weight.astype(jnp.float32)
    centre = beside_all[1:-1].astype(jnp.float32)
    before = beside_all[:-2].astype(jnp.float32)
    following = beside_all[2:].astype(jnp.float32)
    middle = jnp.einsum('tc,cjo->tjo', centre, weight_float[:, half_stride:half_stride + stride])
    earlier = jnp.einsum('tc,cjo->tjo', before, weight_float[:, half_stride + stride:])
    later = jnp.einsum('tc,cjo->tjo', following, weight_float[:, :half_stride])
    combined = middle + jnp.concatenate([earlier, later], axis=1)
    return combined.reshape(-1, weight.shape[2])

def reference(queries, key_rows, value_rows, residual, branch_gate, out_weight, final_scale, final_shift, final_weight, input_conv, lift_slopes, up_weight, unit_slopes, unit_dilated, unit_point):
    split_q = queries.reshape(TOKENS, H, HD).transpose(1, 0, 2)
    split_k = key_rows.reshape(TOKENS, H, HD).transpose(1, 0, 2)
    split_v = value_rows.reshape(TOKENS, H, HD).transpose(1, 0, 2)
    attended = lax.map(one_head, (split_q, split_k, split_v))
    attended = attended.transpose(1, 0, 2).reshape(TOKENS, D)
    projected = jnp.dot(attended, out_weight, preferred_element_type=jnp.float32)
    mixed_rows = residual.astype(jnp.float32) + branch_gate * projected
    row_mean = lax.optimization_barrier(jnp.mean(mixed_rows, axis=1, keepdims=True))
    centred = mixed_rows - row_mean
    variance = lax.optimization_barrier(jnp.mean(centred * centred, axis=1, keepdims=True))
    normed = (centred * lax.rsqrt(variance + 1e-06) * final_scale + final_shift).astype(jnp.bfloat16)
    latent = jnp.dot(normed, final_weight, preferred_element_type=jnp.float32).astype(jnp.bfloat16)
    padded = jnp.pad(latent, ((3, 3), (0, 0)))
    opened = dilated(padded, input_conv, 1, TOKENS)
    lifted = snake(opened, lift_slopes).astype(jnp.bfloat16)
    beside_all = jnp.pad(lifted, ((1, 1), (0, 0)))
    stream = upsample(beside_all, up_weight)
    for unit_index in range(3):
        spread = 3 ** unit_index
        entering = snake(stream, unit_slopes[unit_index, 0]).astype(jnp.bfloat16)
        entering = jnp.pad(entering, ((3 * spread, 3 * spread), (0, 0)))
        widened = dilated(entering, unit_dilated[unit_index], spread, NT)
        inner_field = snake(widened, unit_slopes[unit_index, 1]).astype(jnp.bfloat16)
        stream = stream + jnp.dot(inner_field, unit_point[unit_index], preferred_element_type=jnp.float32)
    return (latent, stream)
```

```python
import functools
import math

import jax
import jax.numpy as jnp
from jax import lax
from jax.experimental import pallas as pl
from jax.experimental.pallas import tpu as pltpu
from jax.sharding import PartitionSpec as P

HD = 64
LOG2E = 1.4426950408889634
SINE = (9.869524955749512, -32.46514129638672, 42.64342498779297, -29.426273345947266, 10.581296920776367)
BF = jnp.bfloat16
F32 = jnp.float32
REACH = 5
EXTRA = REACH + 4
MIB = 2**20


def turns(slopes):
    return slopes * (1.0 / math.pi), 1.0 / slopes


def snake(signal, per_turn, inverse):
    part = signal * per_turn
    part = part - jnp.round(part)
    z = part * part
    poly = SINE[4]
    for c in SINE[3::-1]:
        poly = poly * z + c
    return signal + poly * z * inverse


def three_parts(x):
    high = lax.reduce_precision(x, 8, 7)
    mid = lax.reduce_precision(x - high, 8, 7)
    low = x - high - mid
    return high.astype(BF), mid.astype(BF), low.astype(BF)


def attend_kernel(q_refs, kv_refs, out_refs, k_scr, v_scr):
    heads = 3
    piece = kv_refs[0].shape[1]
    lane = lax.broadcasted_iota(jnp.int32, (piece, 128), 1)
    for h in range(heads):
        for i, kv in enumerate(kv_refs):
            cols = slice(i * piece, (i + 1) * piece)
            key_part = kv[h * HD : (h + 1) * HD, :]
            k_scr[h, :HD, cols] = key_part
            k_scr[h, HD:, cols] = key_part
            values = kv[(heads + h) * HD : (heads + h + 1) * HD, :].astype(F32)
            values = jnp.concatenate([values, jnp.ones_like(values)], axis=0).T
            v_scr[h, cols, :] = jnp.where(lane <= HD, values, 0.0).astype(BF)
    rows = 256
    for q_ref, out_ref in zip(q_refs, out_refs):

        def step(block, carry, q_ref=q_ref, out_ref=out_ref):
            cols = pl.ds(pl.multiple_of(block * rows, rows), rows)
            row_id = lax.broadcasted_iota(jnp.int32, (16, rows), 0)
            stats = jnp.zeros((16, rows), F32)
            for h in range(heads):
                query = q_ref[h * HD : (h + 1) * HD, cols].astype(F32) * (LOG2E / math.sqrt(HD))
                high = query.astype(BF).astype(F32)
                both = jnp.concatenate([high, query - high], axis=0).T.astype(BF)
                scores = [
                    jnp.dot(
                        both,
                        k_scr[h, :, i * piece : (i + 1) * piece],
                        preferred_element_type=F32,
                    )
                    for i in range(len(kv_refs))
                ]
                top = functools.reduce(jnp.maximum, scores)
                top = jnp.max(top, axis=1, keepdims=True)
                total = jnp.zeros((rows, 128), F32)
                for i, s in enumerate(scores):
                    weights = jnp.exp2(s - top).astype(BF)
                    total = total + jnp.dot(
                        weights,
                        v_scr[h, i * piece : (i + 1) * piece, :],
                        preferred_element_type=F32,
                    )
                lanes = lax.broadcasted_iota(jnp.int32, (rows, 128), 1)
                total = jnp.where(lanes == HD + 1, top, total).T
                weight_sum = total[HD : HD + 1]
                level = total[HD + 1 : HD + 2] + jnp.log2(weight_sum)
                out_ref[h * HD : (h + 1) * HD, cols] = (total[:HD] / weight_sum).astype(BF)
                first = level.astype(BF).astype(F32)
                second = (level - first).astype(BF).astype(F32)
                third = level - first - second
                for k, part in enumerate((first, second, third)):
                    stats = jnp.where(row_id == 3 * h + k, part, stats)
            out_ref[heads * HD :, cols] = stats.astype(BF)
            return carry

        lax.fori_loop(0, q_ref.shape[1] // rows, step, 0)


def attend(q_parts, kv_parts):
    n, m = len(q_parts), len(kv_parts)
    piece = kv_parts[0].shape[1]

    def body(*refs):
        attend_kernel(refs[:n], refs[n : n + m], refs[n + m : n + m + n], *refs[n + m + n :])

    vmem = pl.BlockSpec(memory_space=pltpu.VMEM)
    return pl.pallas_call(
        body,
        out_shape=[jax.ShapeDtypeStruct((3 * HD + 16, q.shape[1]), BF) for q in q_parts],
        in_specs=[vmem] * (n + m),
        out_specs=[vmem] * n,
        scratch_shapes=[
            pltpu.VMEM((3, 2 * HD, m * piece), BF),
            pltpu.VMEM((3, m * piece, 128), BF),
        ],
        compiler_params=pltpu.CompilerParams(vmem_limit_bytes=48 * MIB),
        name="attend",
    )(*q_parts, *kv_parts)


def merge(parts):
    levels = []
    for part in parts:
        stat = part[3 * HD : 3 * HD + 9].astype(F32).reshape(3, 3, -1)
        levels.append(stat.sum(axis=1))
    top = functools.reduce(jnp.maximum, levels)
    shares = [jnp.exp2(level - top) for level in levels]
    whole = functools.reduce(jnp.add, shares)
    total = 0.0
    for part, share in zip(parts, shares):
        total = total + part[: 3 * HD].astype(F32).reshape(3, HD, -1) * (share / whole)[:, None]
    return total.reshape(3 * HD, -1).astype(BF)


def units_kernel(taps, where_ref, parts, weights, slopes, outs, stream, w_scr, wide, sems):
    me, first = where_ref[0], where_ref[1]
    rows = stream.shape[0]
    depth = 512

    def fetch(u, t):
        return pltpu.make_async_copy(
            weights.at[t, pl.ds(u * (taps + 1) * depth, (taps + 1) * depth)],
            w_scr.at[u, :, pl.ds(t * 128, 128)],
            sems.at[u, t],
        )

    for u in range(3):
        for t in range(4):
            fetch(u, t).start()
    for t in range(4):

        @pl.when(me == t)
        def _(t=t):
            for k in range(4):
                b = t ^ k
                stream[:, b * 128 : (b + 1) * 128] = parts[k][...].astype(F32)

    step = first + lax.broadcasted_iota(jnp.int32, (rows, depth), 0)
    inside = (step >= 0) & (step < 65536)
    wide[...] = jnp.zeros_like(wide)
    for u in range(3):
        spread = 3**u
        per_turn, inverse = turns(slopes[u, 0:1, :])
        entering = snake(stream[...], per_turn, inverse)
        held = jnp.where(inside, entering, 0.0).astype(BF).astype(F32)
        pad = 3 * spread
        for k in range(taps):
            shift = (k - 3) * spread
            lo, hi = max(0, -shift), min(rows, rows - shift)
            moved = held[lo + shift : hi + shift]
            if lo > 0:
                moved = jnp.concatenate([jnp.zeros((lo, depth), F32), moved], axis=0)
            if hi < rows:
                moved = jnp.concatenate([moved, jnp.zeros((rows - hi, depth), F32)], axis=0)
            wide[:, k * depth : (k + 1) * depth] = moved.astype(BF)
        for t in range(4):
            fetch(u, t).wait()
        widened = jnp.dot(wide[...], w_scr[u, : taps * depth, :], preferred_element_type=F32)
        per_turn, inverse = turns(slopes[u, 1:2, :])
        inner = snake(widened, per_turn, inverse).astype(BF)
        stream[...] += jnp.dot(inner, w_scr[u, taps * depth :, :], preferred_element_type=F32)
    skip = 8 * REACH
    for t in range(4):

        @pl.when(me == t)
        def _(t=t):
            for k in range(4):
                b = t ^ k
                outs[k][...] = stream[skip : skip + 512, b * 128 : (b + 1) * 128].astype(BF)


def units(where, parts, weights, slopes, taps):
    rows = parts[0].shape[0]
    depth = 512

    def body(where_ref, a, b, c, d, w, s, o0, o1, o2, o3, *scr):
        units_kernel(taps, where_ref, (a, b, c, d), w, s, (o0, o1, o2, o3), *scr)

    vmem = pl.BlockSpec(memory_space=pltpu.VMEM)
    return pl.pallas_call(
        body,
        out_shape=[jax.ShapeDtypeStruct((512, 128), BF)] * 4,
        in_specs=[pl.BlockSpec(memory_space=pltpu.SMEM)]
        + [vmem] * 4
        + [pl.BlockSpec(memory_space=pl.ANY), vmem],
        out_specs=[vmem] * 4,
        scratch_shapes=[
            pltpu.VMEM((rows, depth), F32),
            pltpu.VMEM((3, (taps + 1) * depth, depth), BF),
            pltpu.VMEM((rows, taps * depth), BF),
            pltpu.SemaphoreType.DMA((3, 4)),
        ],
        compiler_params=pltpu.CompilerParams(vmem_limit_bytes=56 * MIB),
        name="units",
    )(where, *parts, weights, slopes)


def finish_rows(projected, residual, branch_gate, final_scale, final_shift, final_weight):
    mixed_rows = residual.astype(F32) + branch_gate * projected
    row_mean = jnp.mean(mixed_rows, axis=1, keepdims=True)
    centred = mixed_rows - row_mean
    variance = jnp.mean(centred * centred, axis=1, keepdims=True)
    normed = (centred * lax.rsqrt(variance + 1e-06) * final_scale + final_shift).astype(BF)
    return jnp.dot(normed, final_weight, preferred_element_type=F32).astype(BF)


def upsample(lifted, weight):
    stride = weight.shape[1] // 2
    half = stride // 2
    mul = functools.partial(jnp.einsum, "tc,cjo->tjo", preferred_element_type=F32)
    middle = mul(lifted[1:-1], weight[:, half : half + stride])
    earlier = mul(lifted[:-2], weight[:, half + stride :])
    later = mul(lifted[2:], weight[:, :half])
    whole = middle + jnp.concatenate([earlier, later], axis=1)
    return whole.astype(BF).reshape(-1, weight.shape[2])


def local(
    queries,
    key_rows,
    value_rows,
    residual,
    branch_gate,
    out_weight,
    final_scale,
    final_shift,
    final_weight,
    input_conv,
    lift_slopes,
    up_weight,
    unit_slopes,
    unit_dilated,
    unit_point,
):
    frames = queries.shape[0]
    seq, tp = lax.axis_index("seq"), lax.axis_index("tp")
    low = seq < 16
    z_swap = [(i, i ^ 16) for i in range(32)]

    def along_x(d):
        return [(i, (i & ~3) | ((i + d) & 3)) for i in range(32)]

    def along_y(d):
        return [(i, (i & ~12) | ((i + 4 * d) & 12)) for i in range(32)]

    def across(k):
        return [(i, i ^ k) for i in range(4)]

    out_full = lax.all_gather(out_weight, "tp", axis=0, tiled=True)
    taps = unit_dilated.shape[1]
    flat = jnp.concatenate(
        [unit_dilated, unit_point[:, None]], axis=1
    ).reshape(-1, 128)
    slope_rows = jnp.concatenate(three_parts(unit_slopes.reshape(6, 128)), axis=0)
    flat = jnp.concatenate([flat, jnp.pad(slope_rows, ((0, 14), (0, 0)))], axis=0)
    unit_full = lax.all_gather(flat, "tp", axis=0)
    edge = 3 * (taps + 1) * 512
    slopes = unit_full[:, edge : edge + 18].astype(F32).reshape(4, 3, 6, 128).sum(axis=1)
    slopes = slopes.transpose(1, 0, 2).reshape(3, 2, 512)

    rows_t = jnp.stack([queries.T, key_rows.T, value_rows.T])
    first, second = rows_t[:, : 3 * HD], rows_t[:, 3 * HD :]
    mine = jnp.where(low, first, second)
    theirs = lax.ppermute(jnp.where(low, second, first), "seq", z_swap)
    both = jnp.concatenate([mine, theirs], axis=2)
    q_own = both[0]
    kv_own = both[1:].reshape(6 * HD, -1)
    kv_parts = [kv_own] + [lax.ppermute(kv_own, "seq", along_x(d)) for d in (1, 3, 2)]
    q_parts = [q_own] + [lax.ppermute(q_own, "seq", along_y(d)) for d in (1, 3, 2)]
    out_parts = attend(q_parts, kv_parts)
    back = [out_parts[0]] + [
        lax.ppermute(o, "seq", along_y(-d)) for o, d in zip(out_parts[1:], (1, 3, 2))
    ]
    attended = merge(back)
    mine, theirs = attended[:, :frames], attended[:, frames:]
    theirs = lax.ppermute(theirs, "seq", z_swap)
    attended = jnp.concatenate(
        [jnp.where(low, mine, theirs), jnp.where(low, theirs, mine)], axis=0
    )
    attended = lax.all_gather(attended, "tp", axis=0, tiled=True)
    projected = lax.dot_general(
        attended, out_full, (((0,), (0,)), ((), ())), preferred_element_type=F32
    )
    latent = finish_rows(projected, residual, branch_gate, final_scale, final_shift, final_weight)

    up = [(i, i + 1) for i in range(31)]
    down = [(i + 1, i) for i in range(31)]
    before = lax.ppermute(latent[-EXTRA:], "seq", up)
    after = lax.ppermute(latent[:EXTRA], "seq", down)
    wide = jnp.concatenate([before, latent, after], axis=0)
    count = frames + 2 * EXTRA - 6
    columns = jnp.concatenate([wide[k : k + count] for k in range(7)], axis=1)
    opened = jnp.dot(
        columns, input_conv.reshape(-1, input_conv.shape[2]), preferred_element_type=F32
    )
    position = seq * frames - (EXTRA - 3) + jnp.arange(count)
    inside = (position >= 0) & (position < 8192)
    lifted = snake(opened, *turns(lift_slopes))
    lifted = jnp.where(inside[:, None], lifted, 0.0).astype(BF)
    stream = upsample(lifted, up_weight)
    share = 2 * frames
    window = share + 16 * REACH

    def piece(k):
        return lax.dynamic_slice_in_dim(stream, (tp ^ k) * share, window, axis=0)

    parts = [piece(0)] + [lax.ppermute(piece(k), "tp", across(k)) for k in (1, 2, 3)]
    where = jnp.stack([tp, seq * 8 * frames + tp * share - 8 * REACH]).astype(jnp.int32)
    done = units(where, parts, unit_full, slopes, taps)
    done = [done[0]] + [lax.ppermute(done[k], "tp", across(k)) for k in (1, 2, 3)]
    ordered = []
    for b in range(4):
        chosen = done[b]
        for t in range(1, 4):
            chosen = jnp.where(tp == t, done[t ^ b], chosen)
        ordered.append(chosen)
    decoded = jnp.concatenate(ordered, axis=0).astype(F32)
    return (latent, decoded)


def solution(mesh):
    placed = (
        P("seq", "tp"),
        P("seq", "tp"),
        P("seq", "tp"),
        P("seq", None),
        P(),
        P("tp", None),
        P(),
        P(),
        P(),
        P(),
        P(),
        P(None, None, "tp"),
        P(None, None, "tp"),
        P(None, None, None, "tp"),
        P(None, None, "tp"),
    )
    return jax.shard_map(
        local,
        mesh=mesh,
        in_specs=placed,
        out_specs=(P("seq", None), P("seq", "tp")),
        check_vma=False,
    )
```

```python
import functools
import math

import jax
import jax.numpy as jnp
from jax import lax
from jax.experimental import pallas as pl
from jax.experimental.pallas import tpu as pltpu
from jax.sharding import PartitionSpec as P

HD = 64
LOG2E = 1.4426950408889634
SINE = (9.869524955749512, -32.46514129638672, 42.64342498779297, -29.426273345947266, 10.581296920776367)
BF = jnp.bfloat16
F32 = jnp.float32
REACH = 5
FRAMES = 80
EXTRA = REACH + 4
MIB = 2**20
TOKEN = jax.ShapeDtypeStruct((8, 128), F32)


def turns(slopes):
    return slopes * (1.0 / math.pi), 1.0 / slopes


def snake(signal, per_turn, inverse):
    part = signal * per_turn
    part = part - jnp.round(part)
    z = part * part
    poly = SINE[4]
    for c in SINE[3::-1]:
        poly = poly * z + c
    return signal + poly * z * inverse


def three_parts(x):
    high = lax.reduce_precision(x, 8, 7)
    mid = lax.reduce_precision(x - high, 8, 7)
    low = x - high - mid
    return high.astype(BF), mid.astype(BF), low.astype(BF)


HEADS = 3
CARRY = HD + 8


def plain(body, shapes, inputs, name, vmem=12, scratch=(), flops=0, spaces=None):
    space = {"smem": pltpu.SMEM, "any": pl.ANY}
    specs = [
        pl.BlockSpec(memory_space=space.get((spaces or {}).get(i), pltpu.VMEM))
        for i in range(len(inputs))
    ]
    return pl.pallas_call(
        body,
        out_shape=[jax.ShapeDtypeStruct(s.shape, s.dtype) for s in shapes],
        in_specs=specs,
        out_specs=[pl.BlockSpec(memory_space=pltpu.VMEM)] * len(shapes),
        scratch_shapes=list(scratch),
        cost_estimate=pl.CostEstimate(flops=flops // 16, bytes_accessed=2**16, transcendentals=0),
        compiler_params=pltpu.CompilerParams(vmem_limit_bytes=vmem * MIB),
        name=name,
    )(*inputs)


def split_kernel(where, q, k, v, mine, theirs, scr, sems):
    width = HEADS * HD
    copies = [pltpu.make_async_copy(r, scr.at[n], sems.at[n]) for n, r in enumerate((q, k, v))]
    for copy in copies:
        copy.start()
    for n, copy in enumerate(copies):
        copy.wait()
        turned = scr[n].astype(F32).T.astype(BF)
        rows = slice(n * width, (n + 1) * width)
        for z in range(2):

            @pl.when(where[2] == z)
            def _(z=z, rows=rows, turned=turned):
                mine[rows, :] = turned[z * width : (z + 1) * width]
                theirs[rows, :] = turned[(1 - z) * width : (2 - z) * width]


def join_kernel(mine, theirs, _, out, token):
    token[...] = jnp.zeros_like(token)
    half = mine.shape[1]
    out[:, :half] = mine[HEADS * HD :, :]
    out[:, half:] = theirs[HEADS * HD :, :]


def first_kernel(mine, theirs, _, q_out):
    half = mine.shape[1]
    q_out[:, :half] = mine[: HEADS * HD, :]
    q_out[:, half:] = theirs[: HEADS * HD, :]


def prepare_kernel(kv, k_out, v_out):
    piece = kv.shape[1]
    width = HEADS * HD
    for h in range(HEADS):
        key_part = kv[h * HD : (h + 1) * HD, :]
        k_out[h, :HD, :] = key_part
        k_out[h, HD:, :] = key_part
    values = kv[width:, :].astype(F32)
    first = values[: 2 * HD].T
    last = jnp.concatenate([values[2 * HD :], jnp.zeros((HD, piece), F32)], axis=0).T
    lane = lax.broadcasted_iota(jnp.int32, (piece, 2 * HD), 1)
    ones = jnp.where(lane == HD, 1.0, 0.0)
    v_out[0] = jnp.where(lane < HD, first, ones).astype(BF)
    v_out[1] = jnp.where(lane >= HD, first, jnp.where(lane == 0, 1.0, 0.0)).astype(BF)
    v_out[2] = jnp.where(lane < HD, last, ones).astype(BF)


def prepared(kv):
    piece = kv.shape[1]
    return [
        jax.ShapeDtypeStruct((HEADS, 2 * HD, piece), BF),
        jax.ShapeDtypeStruct((HEADS, piece, 2 * HD), BF),
    ]


def prepare(kv, after):
    def body(kv, _, k_out, v_out):
        prepare_kernel(kv, k_out, v_out)

    return plain(body, prepared(kv), [kv, after], "prepare", flops=10**9, spaces={1: "any"})


def attend_kernel(where, q_all, steps, k_refs, v_refs, c_refs, out_refs, last):
    rows = 256
    row_id = lax.broadcasted_iota(jnp.int32, (16, rows), 0)
    items = [
        (n, block, h)
        for n in range(len(steps))
        for block in range(q_all.shape[2] // rows)
        for h in range(HEADS)
    ]

    def score(n, block, h):
        cols = slice(block * rows, (block + 1) * rows)
        query = q_all[(where[4] - steps[n]) & 3, h * HD : (h + 1) * HD, cols]
        query = query.astype(F32) * (LOG2E / math.sqrt(HD))
        high = query.astype(BF).astype(F32)
        both = jnp.concatenate([high, query - high], axis=0).T.astype(BF)
        return [jnp.dot(both, k[h], preferred_element_type=F32) for k in k_refs]

    def finish(n, block, h, scores, stats):
        cols = slice(block * rows, (block + 1) * rows)
        top = functools.reduce(jnp.maximum, scores)
        top = jnp.max(top, axis=1, keepdims=True)
        total = None
        for s, v in zip(scores, v_refs):
            weights = jnp.exp2(s - top).astype(BF)
            part = jnp.dot(weights, v[h], preferred_element_type=F32)
            total = part if total is None else total + part
        lanes = lax.broadcasted_iota(jnp.int32, (rows, 2 * HD), 1)
        spare = 0 if h == 1 else HD
        total = jnp.where(lanes == spare + 1, top, total).T
        sums = total[HD - spare : 2 * HD - spare]
        weight_sum, top = total[spare : spare + 1], total[spare + 1 : spare + 2]
        if not last:
            out_refs[n][h * CARRY : h * CARRY + HD, cols] = sums
            out_refs[n][h * CARRY + HD : (h + 1) * CARRY, cols] = jnp.where(
                row_id[:8] == 0, weight_sum, top
            )
            return stats
        if c_refs:
            at = h * CARRY
            older_sum = c_refs[n][at + HD : at + HD + 1, cols]
            older = c_refs[n][at + HD + 1 : at + HD + 2, cols]
            newer, top = top, jnp.maximum(top, older)
            here, there = jnp.exp2(newer - top), jnp.exp2(older - top)
            sums = sums * here + c_refs[n][at : at + HD, cols] * there
            weight_sum = weight_sum * here + older_sum * there
        level = top + jnp.log2(weight_sum)
        out_refs[n][h * HD : (h + 1) * HD, cols] = (sums / weight_sum).astype(BF)
        first = level.astype(BF).astype(F32)
        second = (level - first).astype(BF).astype(F32)
        third = level - first - second
        for k, part in enumerate((first, second, third)):
            stats = jnp.where(row_id == 3 * h + k, part, stats)
        if h == HEADS - 1:
            out_refs[n][HEADS * HD :, cols] = stats.astype(BF)
            stats = jnp.zeros_like(stats)
        return stats

    stats = jnp.zeros((16, rows), F32)
    ahead = score(*items[0])
    for i, item in enumerate(items):
        scores = ahead
        if i + 1 < len(items):
            ahead = score(*items[i + 1])
        stats = finish(*item, scores, stats)


def attend(where, q_all, steps, ready, carries=(), last=True, after=()):
    n, m, c = len(steps), len(ready), len(carries)

    def body(where, q_all, *refs):
        ends = (m, 2 * m, 2 * m + c)
        groups = [refs[a:b] for a, b in zip((0,) + ends[:-1], ends)]
        attend_kernel(where, q_all, steps, *groups, refs[ends[-1] + len(after) :], last)

    inputs = [where, q_all] + [r[0] for r in ready] + [r[1] for r in ready] + list(carries)
    rows, kind = (HEADS * HD + 16, BF) if last else (HEADS * CARRY, F32)
    spaces = {len(inputs) + i: "any" for i in range(len(after))}
    return plain(
        body,
        [jax.ShapeDtypeStruct((rows, q_all.shape[2]), kind)] * n,
        inputs + list(after),
        "attend",
        vmem=18,
        flops=int(1.5e9) * n * m,
        spaces={0: "smem", **spaces},
    )


def merge_kernel(p0, p1, p2, p3, mine, theirs):
    parts = [p[...].astype(F32) for p in (p0, p1, p2, p3)]
    half = mine.shape[1]
    for h in range(HEADS):
        levels = []
        for p in parts:
            r = HEADS * HD + 3 * h
            levels.append(p[r : r + 1] + p[r + 1 : r + 2] + p[r + 2 : r + 3])
        top = functools.reduce(jnp.maximum, levels)
        shares = [jnp.exp2(level - top) for level in levels]
        whole = functools.reduce(jnp.add, shares)
        rows = slice(h * HD, (h + 1) * HD)
        total = functools.reduce(jnp.add, [p[rows] * (s / whole) for p, s in zip(parts, shares)])
        mine[rows, :] = total[:, :half].astype(BF)
        theirs[rows, :] = total[:, half:].astype(BF)


def merge(parts):
    shape = jax.ShapeDtypeStruct((HEADS * HD, parts[0].shape[1] // 2), BF)
    return plain(merge_kernel, [shape, shape], parts, "merge", flops=10**9)


def rows_kernel(where, mine, far, out):
    near_z = where[2]
    for z in range(2):

        @pl.when(near_z == z)
        def _(z=z):
            pair = (far, mine) if z else (mine, far)
            both = jnp.concatenate([p[...].astype(F32) for p in pair], axis=0)
            out[...] = both.T.astype(BF)


def project_kernel(
    where, attended, w0, w1, w2, w3, residual, gate, scale, shift, final, out, scr, held, sems
):
    copies = [
        pltpu.make_async_copy(w, scr.at[k], sems.at[k]) for k, w in enumerate((w0, w1, w2, w3))
    ]
    copies.append(pltpu.make_async_copy(residual, held, sems.at[4]))
    for copy in copies:
        copy.start()
    total = None
    for k in range(4):
        copies[k].wait()
        part = jnp.dot(attended[where[0] ^ k], scr[k], preferred_element_type=F32)
        total = part if total is None else total + part
    copies[4].wait()
    mixed = held[...].astype(F32) + gate[...] * total
    mean = jnp.mean(mixed, axis=1, keepdims=True)
    centred = mixed - mean
    variance = jnp.mean(centred * centred, axis=1, keepdims=True)
    normed = (centred * lax.rsqrt(variance + 1e-06) * scale[...] + shift[...]).astype(BF)
    out[...] = jnp.dot(normed, final[...], preferred_element_type=F32).astype(BF)


def project(where, attended, weights, residual, gate, scale, shift, final):
    shape = jax.ShapeDtypeStruct((residual.shape[0], final.shape[1]), BF)
    inputs = [where, attended, *weights, residual, gate[None], scale[None], shift[None], final]
    return plain(
        project_kernel,
        [shape],
        inputs,
        "project",
        vmem=60,
        flops=4 * 10**9,
        spaces={0: "smem", **{i: "any" for i in range(2, 7)}},
        scratch=[
            pltpu.VMEM((4,) + weights[0].shape, BF),
            pltpu.VMEM(residual.shape, BF),
            pltpu.SemaphoreType.DMA((5,)),
        ],
    )[0]


def raise_kernel(where, before, latent, after, conv, bend, up, *refs):
    outs = refs[:4]
    wide, columns, conv_scr, raw, up_scr, lifted, taps, stream, sems = refs[4:]
    depth_up, count, channels = up.shape
    parts = 8
    block = depth_up // parts
    places = [pl.ds(i * block, block) for i in range(parts)]
    ins = [pltpu.make_async_copy(up.at[p], raw.at[p], sems.at[i]) for i, p in enumerate(places)]
    conv_in = pltpu.make_async_copy(conv, conv_scr, sems.at[parts])
    conv_in.start()
    for copy in ins:
        copy.start()
    size = count * count
    to = lax.broadcasted_iota(jnp.int32, (size, size), 0)
    of = lax.broadcasted_iota(jnp.int32, (size, size), 1)
    swap = jnp.where(of == (to % count) * count + to // count, 1.0, 0.0).astype(BF)

    def turn(i):
        ins[i].wait()
        for c in range(i * block, (i + 1) * block, 2 * count):
            pair = [
                raw[c + n * count : c + (n + 1) * count].reshape(size, channels) for n in range(2)
            ]
            pair = jnp.concatenate(pair, axis=1)
            moved = jnp.dot(swap, pair, preferred_element_type=F32).astype(BF)
            for n in range(2):
                for j in range(count):
                    up_scr[
                        c + n * count : c + (n + 1) * count, j * channels : (j + 1) * channels
                    ] = moved[j * count : (j + 1) * count, n * channels : (n + 1) * channels]

    rows = columns.shape[0]
    frames, width = latent.shape
    wide[...] = jnp.zeros_like(wide)
    wide[:EXTRA, :width] = before[...].astype(F32)
    wide[EXTRA : EXTRA + frames, :width] = latent[...].astype(F32)
    wide[EXTRA + frames : 2 * EXTRA + frames, :width] = after[...].astype(F32)
    for k in range(0, 8, 2):
        pair = wide[k : k + rows, :]
        if k < 6:
            pair = pair + pltpu.roll(wide[k + 1 : k + 1 + rows, :], width, 1)
        columns[:, k * width : (k + 2) * width] = pair.astype(BF)
    step = 512
    frame = where[3] + lax.broadcasted_iota(jnp.int32, (rows, step), 0)
    inside = (frame >= 0) & (frame < 8192)
    conv_in.wait()
    depth = conv.shape[0]
    for c in range(0, lifted.shape[1], step):
        cols = slice(c, c + step)
        opened = jnp.dot(columns[:, :depth], conv_scr[:, cols], preferred_element_type=F32)
        up_part = snake(opened, *turns(bend[:, cols]))
        lifted[:, cols] = jnp.where(inside, up_part, 0.0).astype(BF)
        turn(c // step * 2)
        turn(c // step * 2 + 1)
    taps[rows:, :] = jnp.zeros((taps.shape[0] - rows, taps.shape[1]), F32)
    for c in range(0, taps.shape[1], step):
        cols = slice(c, c + step)
        taps[:rows, cols] = jnp.dot(lifted[...], up_scr[:, cols], preferred_element_type=F32)
    before_part = taps[0:rows, 3 * step :]
    after_part = taps[2 : 2 + rows, :step]
    stream[:, :step] = (taps[1 : 1 + rows, step : 2 * step] + before_part).astype(BF)
    stream[:, step:] = (taps[1 : 1 + rows, 2 * step : 3 * step] + after_part).astype(BF)
    for k, out in enumerate(outs):
        start = pl.multiple_of((where[0] ^ k) * 64, 64)
        out[...] = stream[pl.ds(start, out.shape[0]), :]


def raise_frames(where, before, latent, after, conv, bend, up):
    rows, depth = latent.shape[0] + 16, conv.shape[1]
    width = up.shape[1] * up.shape[2]
    shape = jax.ShapeDtypeStruct((FRAMES, width // 2), BF)
    return plain(
        raise_kernel,
        [shape] * 4,
        [where, before, latent, after, conv, bend[None], up],
        "raise",
        vmem=60,
        flops=6 * 10**9,
        spaces={0: "smem", 4: "any", 6: "any"},
        scratch=[
            pltpu.VMEM((rows + 8, 2 * latent.shape[1]), F32),
            pltpu.VMEM((rows, 8 * latent.shape[1]), BF),
            pltpu.VMEM(conv.shape, BF),
            pltpu.VMEM(up.shape, BF),
            pltpu.VMEM((depth, width), BF),
            pltpu.VMEM((rows, depth), BF),
            pltpu.VMEM((rows + 8, width), F32),
            pltpu.VMEM((rows, width // 2), BF),
            pltpu.SemaphoreType.DMA((9,)),
        ],
    )


def units_kernel(taps, where_ref, parts, w_scr, slopes, outs, *scr):
    stream, held, wides = scr[0], scr[1], scr[2:4]
    me, first = where_ref[0], where_ref[1]
    depth = 512
    frames = parts[0].shape[0]

    held[...] = jnp.zeros_like(held)
    for t in range(4):

        @pl.when(me == t)
        def _(t=t):
            for k in range(4):
                cols = slice((t ^ k) * 128, ((t ^ k) + 1) * 128)
                for j in range(8):
                    piece = parts[k][:, j * 128 : (j + 1) * 128]
                    stream[j * frames : (j + 1) * frames, cols] = piece.astype(F32)

    row = lax.broadcasted_iota(jnp.int32, (frames, depth), 0)
    for u in range(3):
        spread = 3**u
        per_turn, inverse = turns(slopes[2 * u : 2 * u + 1, :])
        for j in range(8):
            step = first + j + 8 * row
            inside = (step >= 0) & (step < 65536)
            entering = snake(stream[j * frames : (j + 1) * frames, :], per_turn, inverse)
            held[j, 8 : 8 + frames, :] = jnp.where(inside, entering, 0.0)
        per_turn, inverse = turns(slopes[2 * u + 1 : 2 * u + 2, :])
        for half, wide in enumerate(wides):
            for m in range(-3 * spread, 8 + 3 * spread):
                spots = []
                for k in range(taps):
                    j = m - (k - 3) * spread - 4 * half
                    if 0 <= j < 4:
                        spots.append((j, k))
                if spots:
                    start = 8 + m // 8
                    moved = held[m % 8, start : start + frames, :].astype(BF)
                    for j, k in spots:
                        wide[j * frames : (j + 1) * frames, k * depth : (k + 1) * depth] = moved
            widened = jnp.dot(
                wide[...], w_scr[u, :taps].reshape(taps * depth, depth), preferred_element_type=F32
            )
            inner = snake(widened, per_turn, inverse).astype(BF)
            rows = slice(half * 4 * frames, (half + 1) * 4 * frames)
            stream[rows, :] += jnp.dot(
                inner, w_scr[u, taps], preferred_element_type=F32
            )
    for t in range(4):

        @pl.when(me == t)
        def _(t=t):
            for k in range(4):
                cols = slice((t ^ k) * 128, ((t ^ k) + 1) * 128)
                for j in range(8):
                    start = j * frames + REACH
                    piece = stream[start : start + 64, cols]
                    outs[k][:, j * 128 : (j + 1) * 128] = piece.astype(BF)


def assemble_kernel(taps, where, *refs):
    parts, (out, slopes, bends, sems, bend_sems) = refs[:4], refs[4:]
    depth = out.shape[2]

    def move(u, k):
        cols = pl.ds(pl.multiple_of((where[0] ^ k) * 128, 128), 128)
        return pltpu.make_async_copy(
            parts[k].at[pl.ds(u * (taps + 1), taps + 1)],
            out.at[u, pl.ds(0, taps + 1), :, cols],
            sems.at[u, k],
        )

    def bend_move(k):
        return pltpu.make_async_copy(
            parts[k].at[3 * (taps + 1), pl.ds(0, 32)], bends.at[k], bend_sems.at[k]
        )

    for k in range(4):
        bend_move(k).start()
    for u in range(3):
        for k in range(4):
            move(u, k).start()
    for k in range(4):
        bend_move(k).wait()
    for t in range(4):

        @pl.when(where[0] == t)
        def _(t=t):
            for k in range(4):
                cols = slice((t ^ k) * 128, ((t ^ k) + 1) * 128)
                bend = bends[k].astype(F32)
                slopes[:, cols] = bend[:8] + bend[8:16] + bend[16:24]

    for u in range(3):
        for k in range(4):
            move(u, k).wait()


def assemble(where, weights, taps):
    depth = weights[0].shape[1]
    shapes = [
        jax.ShapeDtypeStruct((3, taps + 1, depth, depth), BF),
        jax.ShapeDtypeStruct((8, depth), F32),
    ]
    spaces = {0: "smem", 1: "any", 2: "any", 3: "any", 4: "any"}
    return plain(
        functools.partial(assemble_kernel, taps),
        shapes,
        [where, *weights],
        "assemble",
        vmem=16,
        flops=6 * 10**9,
        spaces=spaces,
        scratch=[
            pltpu.VMEM((4, 32, 128), BF),
            pltpu.SemaphoreType.DMA((3, 4)),
            pltpu.SemaphoreType.DMA((4,)),
        ],
    )


def units(where, parts, whole, slopes):
    frames = parts[0].shape[0]
    taps, depth = whole.shape[1] - 1, whole.shape[2]

    def body(where_ref, p0, p1, p2, p3, w, s, o0, o1, o2, o3, *scr):
        units_kernel(taps, where_ref, (p0, p1, p2, p3), w, s, (o0, o1, o2, o3), *scr)

    return plain(
        body,
        [jax.ShapeDtypeStruct((64, 1024), BF)] * 4,
        [where, *parts, whole, slopes],
        "units",
        vmem=30,
        flops=12 * 10**9,
        spaces={0: "smem"},
        scratch=[
            pltpu.VMEM((8 * frames, depth), F32),
            pltpu.VMEM((8, frames + 16, depth), F32),
            pltpu.VMEM((4 * frames, taps * depth), BF),
            pltpu.VMEM((4 * frames, taps * depth), BF),
        ],
    )


def place_kernel(where, p0, p1, p2, p3, out):
    frames = p0.shape[0]
    for t in range(4):

        @pl.when(where[0] == t)
        def _(t=t):
            for k, part in enumerate((p0, p1, p2, p3)):
                for j in range(8):
                    rows = pl.ds((t ^ k) * 8 * frames + j, frames, stride=8)
                    out[rows, :] = part[:, j * 128 : (j + 1) * 128].astype(F32)


def pack(dilated, point, bend, after):
    def body(x, y, z, _, out, token, scr, sems):
        token[...] = jnp.zeros_like(token)
        units, taps, depth = x.shape[:3]
        moves = []
        for u in range(units):
            at = u * (taps + 1)
            moves.append((x.at[u], pl.ds(at, taps)))
            moves.append((y.at[pl.ds(u, 1)], pl.ds(at + taps, 1)))
        for i, (source, place) in enumerate(moves):
            pltpu.make_async_copy(source, scr.at[place], sems.at[0, i]).start()
        tail = scr.shape[0] - 1
        scr[tail] = jnp.zeros(scr.shape[1:], BF)
        scr[tail, :24, :] = z[...]
        pltpu.make_async_copy(scr.at[tail], out.at[tail], sems.at[1, len(moves)]).start()
        for i, (source, place) in enumerate(moves):
            pltpu.make_async_copy(source, scr.at[place], sems.at[0, i]).wait()
            pltpu.make_async_copy(scr.at[place], out.at[place], sems.at[1, i]).start()
        for i, (source, place) in enumerate(moves):
            pltpu.make_async_copy(scr.at[place], out.at[place], sems.at[1, i]).wait()
        pltpu.make_async_copy(scr.at[tail], out.at[tail], sems.at[1, len(moves)]).wait()

    anywhere = pl.BlockSpec(memory_space=pl.ANY)
    units, taps, depth, width = dilated.shape
    shape = (units * (taps + 1) + 1, depth, width)
    return pl.pallas_call(
        body,
        out_shape=[jax.ShapeDtypeStruct(shape, BF), TOKEN],
        in_specs=[anywhere] * 2 + [pl.BlockSpec(memory_space=pltpu.VMEM), anywhere],
        out_specs=[anywhere, pl.BlockSpec(memory_space=pltpu.VMEM)],
        scratch_shapes=[pltpu.VMEM(shape, BF), pltpu.SemaphoreType.DMA((2, 7))],
        cost_estimate=pl.CostEstimate(flops=0, bytes_accessed=2**23, transcendentals=0),
        compiler_params=pltpu.CompilerParams(vmem_limit_bytes=60 * MIB),
        name="pack",
    )(dilated, point, bend, after)


def tie(x, *after):
    anywhere = pl.BlockSpec(memory_space=pl.ANY)
    return pl.pallas_call(
        lambda *refs: None,
        out_shape=jax.ShapeDtypeStruct(x.shape, x.dtype),
        in_specs=[anywhere] * (1 + len(after)),
        out_specs=anywhere,
        input_output_aliases={0: 0},
        name="tie",
    )(x, *after)


def local(
    queries,
    key_rows,
    value_rows,
    residual,
    branch_gate,
    out_weight,
    final_scale,
    final_shift,
    final_weight,
    input_conv,
    lift_slopes,
    up_weight,
    unit_slopes,
    unit_dilated,
    unit_point,
):
    frames = queries.shape[0]
    seq, tp = lax.axis_index("seq"), lax.axis_index("tp")
    low = seq < 16
    share = 2 * frames
    begin = seq * frames - (EXTRA - 3)
    where = [tp, seq * 8 * frames + tp * share - 8 * REACH, seq // 16, begin, (seq // 4) % 4]
    where = jnp.stack(where)
    where = where.astype(jnp.int32)

    def along_x(d):
        return [(i, (i & ~3) | ((i + d) & 3)) for i in range(32)]

    def along_y(d):
        return [(i, (i & ~12) | ((i + 4 * d) & 12)) for i in range(32)]

    def across(k):
        return [(i, i ^ k) for i in range(4)]

    def column(z, k):
        return [(4 * i + j, 4 * (i ^ (16 * z)) + (j ^ k)) for i in range(32) for j in range(4)]

    def send_column(x, z, k):
        return lax.ppermute(x, ("seq", "tp"), column(z, k))

    shape = jax.ShapeDtypeStruct((9 * HD, frames), BF)
    mine, theirs = plain(
        split_kernel,
        [shape, shape],
        [where, queries, key_rows, value_rows],
        "split",
        vmem=60,
        spaces={0: "smem", 1: "any", 2: "any", 3: "any"},
        scratch=[pltpu.VMEM((3,) + queries.shape, BF), pltpu.SemaphoreType.DMA((3,))],
    )
    theirs = send_column(theirs, 1, 0)
    taps = unit_dilated.shape[1]
    bend = jnp.concatenate(
        [jnp.pad(p, ((0, 2), (0, 0))) for p in three_parts(unit_slopes.reshape(6, 128))]
    )
    packed, token = pack(unit_dilated, unit_point, bend, mine)
    kv_own, token = plain(
        join_kernel,
        [jax.ShapeDtypeStruct((6 * HD, 2 * frames), BF), TOKEN],
        [mine, theirs, token],
        "join",
        spaces={2: "any"},
    )
    order = (1, 3, 2)
    kv_far = [lax.ppermute(kv_own, "seq", along_x(d)) for d in order]
    (q_own,) = plain(
        first_kernel,
        [jax.ShapeDtypeStruct((3 * HD, 2 * frames), BF)],
        [mine, theirs, token],
        "first",
        spaces={2: "any"},
    )
    ring = [[16 * z + 4 * y + x for y in range(4)] for z in range(2) for x in range(4)]
    q_all = lax.all_gather(q_own, "seq", axis_index_groups=ring)

    out_beyond = send_column(out_weight, 1, 2)
    ready = [prepare(kv, kv) for kv in [kv_own] + kv_far]
    packed = tie(packed, out_beyond, ready[1][0], ready[2][0])
    packed_beyond = send_column(packed, 1, 2)
    carries = attend(where, q_all, order[:2], ready[:3], last=False, after=[packed])
    out_parts = [
        out_weight,
        lax.ppermute(out_weight, "tp", across(1)),
        out_beyond,
        lax.ppermute(out_beyond, "tp", across(1)),
    ]
    out1, out3 = attend(where, q_all, order[:2], ready[3:], carries)
    (out2,) = attend(where, q_all, order[2:], ready, after=[out1])
    after = [out2, out_parts[1], out_parts[3]]
    (out0,) = attend(where, q_all, (0,), ready, after=after)
    back = [lax.ppermute(o, "seq", along_y(-d)) for o, d in zip((out1, out3, out2), order)]
    mine, theirs = merge([out0] + back)
    far = send_column(theirs, 1, 0)
    (attended,) = plain(
        rows_kernel,
        [jax.ShapeDtypeStruct((frames, 6 * HD), BF)],
        [where, mine, far],
        "rows",
        spaces={0: "smem"},
    )
    attended = lax.all_gather(attended, "tp")
    latent = project(
        where, attended, out_parts, residual, branch_gate, final_scale, final_shift, final_weight
    )

    packed_beyond = tie(packed_beyond, latent)
    packed_parts = [packed, lax.ppermute(packed, "tp", across(1)), packed_beyond]
    packed_parts.append(lax.ppermute(packed_beyond, "tp", across(1)))

    up = [(i, i + 1) for i in range(31)]
    down = [(i + 1, i) for i in range(31)]
    before = lax.ppermute(latent[-EXTRA:], "seq", up)
    after = lax.ppermute(latent[:EXTRA], "seq", down)
    conv = input_conv.reshape(-1, input_conv.shape[2])
    parts = raise_frames(where, before, latent, after, conv, lift_slopes, up_weight)
    parts = [parts[0]] + [lax.ppermute(parts[k], "tp", across(k)) for k in (1, 2, 3)]
    done = units(where, parts, *assemble(where, packed_parts, taps))
    done = [done[0]] + [lax.ppermute(done[k], "tp", across(k)) for k in (1, 2, 3)]
    (decoded,) = plain(
        place_kernel,
        [jax.ShapeDtypeStruct((8 * frames, 128), F32)],
        [where, *done],
        "place",
        spaces={0: "smem"},
    )
    return (latent, decoded)


def solution(mesh):
    placed = (
        P("seq", "tp"),
        P("seq", "tp"),
        P("seq", "tp"),
        P("seq", None),
        P(),
        P("tp", None),
        P(),
        P(),
        P(),
        P(),
        P(),
        P(None, None, "tp"),
        P(None, None, "tp"),
        P(None, None, None, "tp"),
        P(None, None, "tp"),
    )
    return jax.shard_map(
        local,
        mesh=mesh,
        in_specs=placed,
        out_specs=(P("seq", None), P("seq", "tp")),
        check_vma=False,
    )
```

```python
import functools
import math

import jax
import jax.numpy as jnp
from jax import lax
from jax.experimental import pallas as pl
from jax.experimental.pallas import tpu as pltpu
from jax.sharding import PartitionSpec as P

HD = 64
LOG2E = 1.4426950408889634
SINE = (9.869524955749512, -32.46514129638672, 42.64342498779297, -29.426273345947266, 10.581296920776367)
BF = jnp.bfloat16
F32 = jnp.float32
REACH = 5
FRAMES = 80
EXTRA = REACH + 4
MIB = 2**20
TOKEN = jax.ShapeDtypeStruct((8, 128), F32)


def turns(slopes):
    return slopes * (1.0 / math.pi), 1.0 / slopes


def snake(signal, per_turn, inverse):
    part = signal * per_turn
    part = part - jnp.round(part)
    z = part * part
    poly = SINE[4]
    for c in SINE[3::-1]:
        poly = poly * z + c
    return signal + poly * z * inverse


def three_parts(x):
    high = lax.reduce_precision(x, 8, 7)
    mid = lax.reduce_precision(x - high, 8, 7)
    low = x - high - mid
    return high.astype(BF), mid.astype(BF), low.astype(BF)


HEADS = 3
CARRY = HD + 8


def plain(body, shapes, inputs, name, vmem=12, scratch=(), flops=0, spaces=None):
    space = {"smem": pltpu.SMEM, "any": pl.ANY}
    specs = [
        pl.BlockSpec(memory_space=space.get((spaces or {}).get(i), pltpu.VMEM))
        for i in range(len(inputs))
    ]
    return pl.pallas_call(
        body,
        out_shape=[jax.ShapeDtypeStruct(s.shape, s.dtype) for s in shapes],
        in_specs=specs,
        out_specs=[pl.BlockSpec(memory_space=pltpu.VMEM)] * len(shapes),
        scratch_shapes=list(scratch),
        cost_estimate=pl.CostEstimate(flops=flops // 16, bytes_accessed=2**16, transcendentals=0),
        compiler_params=pltpu.CompilerParams(vmem_limit_bytes=vmem * MIB),
        name=name,
    )(*inputs)


def split_kernel(where, q, k, v, mine, theirs, scr, sems):
    width = HEADS * HD
    copies = [pltpu.make_async_copy(r, scr.at[n], sems.at[n]) for n, r in enumerate((q, k, v))]
    for copy in copies:
        copy.start()
    for n, copy in enumerate(copies):
        copy.wait()
        turned = scr[n].astype(F32).T.astype(BF)
        rows = slice(n * width, (n + 1) * width)
        for z in range(2):

            @pl.when(where[2] == z)
            def _(z=z, rows=rows, turned=turned):
                mine[rows, :] = turned[z * width : (z + 1) * width]
                theirs[rows, :] = turned[(1 - z) * width : (2 - z) * width]


def join_kernel(mine, theirs, _, out, token):
    token[...] = jnp.zeros_like(token)
    half = mine.shape[1]
    out[:, :half] = mine[HEADS * HD :, :]
    out[:, half:] = theirs[HEADS * HD :, :]


def first_kernel(kv, mine, theirs, q_out, q_again, kv_again):
    kv_again[...] = kv[...]
    half = mine.shape[1]
    for out in (q_out, q_again):
        out[:, :half] = mine[: HEADS * HD, :]
        out[:, half:] = theirs[: HEADS * HD, :]


def prepare_kernel(kv, k_out, v_out):
    piece = kv.shape[1]
    width = HEADS * HD
    for h in range(HEADS):
        key_part = kv[h * HD : (h + 1) * HD, :]
        k_out[h, :HD, :] = key_part
        k_out[h, HD:, :] = key_part
    values = kv[width:, :].astype(F32)
    first = values[: 2 * HD].T
    last = jnp.concatenate([values[2 * HD :], jnp.zeros((HD, piece), F32)], axis=0).T
    lane = lax.broadcasted_iota(jnp.int32, (piece, 2 * HD), 1)
    ones = jnp.where(lane == HD, 1.0, 0.0)
    v_out[0] = jnp.where(lane < HD, first, ones).astype(BF)
    v_out[1] = jnp.where(lane >= HD, first, jnp.where(lane == 0, 1.0, 0.0)).astype(BF)
    v_out[2] = jnp.where(lane < HD, last, ones).astype(BF)


def prepared(kv):
    piece = kv.shape[1]
    return [
        jax.ShapeDtypeStruct((HEADS, 2 * HD, piece), BF),
        jax.ShapeDtypeStruct((HEADS, piece, 2 * HD), BF),
    ]


def prepare(kv):
    def body(kv, k_out, v_out, token):
        token[...] = jnp.zeros_like(token)
        prepare_kernel(kv, k_out, v_out)

    return plain(body, prepared(kv) + [TOKEN], [kv], "prepare", flops=10**9)


def attend_kernel(q_refs, k_refs, v_refs, c_refs, out_refs, last):
    rows = 256
    row_id = lax.broadcasted_iota(jnp.int32, (16, rows), 0)
    items = [
        (n, block, h)
        for n, q in enumerate(q_refs)
        for block in range(q.shape[1] // rows)
        for h in range(HEADS)
    ]

    def score(n, block, h):
        cols = slice(block * rows, (block + 1) * rows)
        query = q_refs[n][h * HD : (h + 1) * HD, cols].astype(F32) * (LOG2E / math.sqrt(HD))
        high = query.astype(BF).astype(F32)
        both = jnp.concatenate([high, query - high], axis=0).T.astype(BF)
        return [jnp.dot(both, k[h], preferred_element_type=F32) for k in k_refs]

    def finish(n, block, h, scores, stats):
        cols = slice(block * rows, (block + 1) * rows)
        top = functools.reduce(jnp.maximum, scores)
        top = jnp.max(top, axis=1, keepdims=True)
        total = None
        for s, v in zip(scores, v_refs):
            weights = jnp.exp2(s - top).astype(BF)
            part = jnp.dot(weights, v[h], preferred_element_type=F32)
            total = part if total is None else total + part
        lanes = lax.broadcasted_iota(jnp.int32, (rows, 2 * HD), 1)
        spare = 0 if h == 1 else HD
        total = jnp.where(lanes == spare + 1, top, total).T
        sums = total[HD - spare : 2 * HD - spare]
        weight_sum, top = total[spare : spare + 1], total[spare + 1 : spare + 2]
        if not last:
            out_refs[n][h * CARRY : h * CARRY + HD, cols] = sums
            out_refs[n][h * CARRY + HD : (h + 1) * CARRY, cols] = jnp.where(
                row_id[:8] == 0, weight_sum, top
            )
            return stats
        if c_refs:
            at = h * CARRY
            older_sum = c_refs[n][at + HD : at + HD + 1, cols]
            older = c_refs[n][at + HD + 1 : at + HD + 2, cols]
            newer, top = top, jnp.maximum(top, older)
            here, there = jnp.exp2(newer - top), jnp.exp2(older - top)
            sums = sums * here + c_refs[n][at : at + HD, cols] * there
            weight_sum = weight_sum * here + older_sum * there
        level = top + jnp.log2(weight_sum)
        out_refs[n][h * HD : (h + 1) * HD, cols] = (sums / weight_sum).astype(BF)
        first = level.astype(BF).astype(F32)
        second = (level - first).astype(BF).astype(F32)
        third = level - first - second
        for k, part in enumerate((first, second, third)):
            stats = jnp.where(row_id == 3 * h + k, part, stats)
        if h == HEADS - 1:
            out_refs[n][HEADS * HD :, cols] = stats.astype(BF)
            stats = jnp.zeros_like(stats)
        return stats

    stats = jnp.zeros((16, rows), F32)
    ahead = score(*items[0])
    for i, item in enumerate(items):
        scores = ahead
        if i + 1 < len(items):
            ahead = score(*items[i + 1])
        stats = finish(*item, scores, stats)


def attend(q_parts, ready, carries=(), last=True, after=()):
    n, m, c = len(q_parts), len(ready), len(carries)

    def body(*refs):
        ends = (n, n + m, n + 2 * m, n + 2 * m + c)
        groups = [refs[a:b] for a, b in zip((0,) + ends[:-1], ends)]
        attend_kernel(*groups, refs[ends[-1] + len(after) :], last)

    inputs = list(q_parts) + [r[0] for r in ready] + [r[1] for r in ready] + list(carries)
    rows, kind = (HEADS * HD + 16, BF) if last else (HEADS * CARRY, F32)
    return plain(
        body,
        [jax.ShapeDtypeStruct((rows, q.shape[1]), kind) for q in q_parts],
        inputs + list(after),
        "attend",
        vmem=18,
        flops=int(1.5e9) * n * m,
        spaces={len(inputs) + i: "any" for i in range(len(after))},
    )


def merge_kernel(p0, p1, p2, p3, mine, theirs):
    parts = [p[...].astype(F32) for p in (p0, p1, p2, p3)]
    half = mine.shape[1]
    for h in range(HEADS):
        levels = []
        for p in parts:
            r = HEADS * HD + 3 * h
            levels.append(p[r : r + 1] + p[r + 1 : r + 2] + p[r + 2 : r + 3])
        top = functools.reduce(jnp.maximum, levels)
        shares = [jnp.exp2(level - top) for level in levels]
        whole = functools.reduce(jnp.add, shares)
        rows = slice(h * HD, (h + 1) * HD)
        total = functools.reduce(jnp.add, [p[rows] * (s / whole) for p, s in zip(parts, shares)])
        mine[rows, :] = total[:, :half].astype(BF)
        theirs[rows, :] = total[:, half:].astype(BF)


def merge(parts):
    shape = jax.ShapeDtypeStruct((HEADS * HD, parts[0].shape[1] // 2), BF)
    return plain(merge_kernel, [shape, shape], parts, "merge", flops=10**9)


def rows_kernel(where, mine, far, out):
    near_z = where[2]
    for z in range(2):

        @pl.when(near_z == z)
        def _(z=z):
            pair = (far, mine) if z else (mine, far)
            both = jnp.concatenate([p[...].astype(F32) for p in pair], axis=0)
            out[...] = both.T.astype(BF)


def project_kernel(
    where, attended, w0, w1, w2, w3, residual, gate, scale, shift, final, out, scr, held, sems
):
    copies = [
        pltpu.make_async_copy(w, scr.at[k], sems.at[k]) for k, w in enumerate((w0, w1, w2, w3))
    ]
    copies.append(pltpu.make_async_copy(residual, held, sems.at[4]))
    for copy in copies:
        copy.start()
    total = None
    for k in range(4):
        copies[k].wait()
        part = jnp.dot(attended[where[0] ^ k], scr[k], preferred_element_type=F32)
        total = part if total is None else total + part
    copies[4].wait()
    mixed = held[...].astype(F32) + gate[...] * total
    mean = jnp.mean(mixed, axis=1, keepdims=True)
    centred = mixed - mean
    variance = jnp.mean(centred * centred, axis=1, keepdims=True)
    normed = (centred * lax.rsqrt(variance + 1e-06) * scale[...] + shift[...]).astype(BF)
    out[...] = jnp.dot(normed, final[...], preferred_element_type=F32).astype(BF)


def project(where, attended, weights, residual, gate, scale, shift, final):
    shape = jax.ShapeDtypeStruct((residual.shape[0], final.shape[1]), BF)
    inputs = [where, attended, *weights, residual, gate[None], scale[None], shift[None], final]
    return plain(
        project_kernel,
        [shape],
        inputs,
        "project",
        vmem=60,
        flops=4 * 10**9,
        spaces={0: "smem", **{i: "any" for i in range(2, 7)}},
        scratch=[
            pltpu.VMEM((4,) + weights[0].shape, BF),
            pltpu.VMEM(residual.shape, BF),
            pltpu.SemaphoreType.DMA((5,)),
        ],
    )[0]


def raise_kernel(where, before, latent, after, conv, bend, up, *refs):
    outs = refs[:4]
    wide, columns, conv_scr, raw, up_scr, lifted, taps, stream, sems = refs[4:]
    depth_up, count, channels = up.shape
    parts = 8
    block = depth_up // parts
    places = [pl.ds(i * block, block) for i in range(parts)]
    ins = [pltpu.make_async_copy(up.at[p], raw.at[p], sems.at[i]) for i, p in enumerate(places)]
    conv_in = pltpu.make_async_copy(conv, conv_scr, sems.at[parts])
    conv_in.start()
    for copy in ins:
        copy.start()
    size = count * count
    to = lax.broadcasted_iota(jnp.int32, (size, size), 0)
    of = lax.broadcasted_iota(jnp.int32, (size, size), 1)
    swap = jnp.where(of == (to % count) * count + to // count, 1.0, 0.0).astype(BF)

    def turn(i):
        ins[i].wait()
        for c in range(i * block, (i + 1) * block, 2 * count):
            pair = [
                raw[c + n * count : c + (n + 1) * count].reshape(size, channels) for n in range(2)
            ]
            pair = jnp.concatenate(pair, axis=1)
            moved = jnp.dot(swap, pair, preferred_element_type=F32).astype(BF)
            for n in range(2):
                for j in range(count):
                    up_scr[
                        c + n * count : c + (n + 1) * count, j * channels : (j + 1) * channels
                    ] = moved[j * count : (j + 1) * count, n * channels : (n + 1) * channels]

    rows = columns.shape[0]
    frames, width = latent.shape
    wide[...] = jnp.zeros_like(wide)
    wide[:EXTRA, :width] = before[...].astype(F32)
    wide[EXTRA : EXTRA + frames, :width] = latent[...].astype(F32)
    wide[EXTRA + frames : 2 * EXTRA + frames, :width] = after[...].astype(F32)
    for k in range(0, 8, 2):
        pair = wide[k : k + rows, :]
        if k < 6:
            pair = pair + pltpu.roll(wide[k + 1 : k + 1 + rows, :], width, 1)
        columns[:, k * width : (k + 2) * width] = pair.astype(BF)
    step = 512
    frame = where[3] + lax.broadcasted_iota(jnp.int32, (rows, step), 0)
    inside = (frame >= 0) & (frame < 8192)
    conv_in.wait()
    depth = conv.shape[0]
    for c in range(0, lifted.shape[1], step):
        cols = slice(c, c + step)
        opened = jnp.dot(columns[:, :depth], conv_scr[:, cols], preferred_element_type=F32)
        up_part = snake(opened, *turns(bend[:, cols]))
        lifted[:, cols] = jnp.where(inside, up_part, 0.0).astype(BF)
        turn(c // step * 2)
        turn(c // step * 2 + 1)
    taps[rows:, :] = jnp.zeros((taps.shape[0] - rows, taps.shape[1]), F32)
    for c in range(0, taps.shape[1], step):
        cols = slice(c, c + step)
        taps[:rows, cols] = jnp.dot(lifted[...], up_scr[:, cols], preferred_element_type=F32)
    before_part = taps[0:rows, 3 * step :]
    after_part = taps[2 : 2 + rows, :step]
    stream[:, :step] = (taps[1 : 1 + rows, step : 2 * step] + before_part).astype(BF)
    stream[:, step:] = (taps[1 : 1 + rows, 2 * step : 3 * step] + after_part).astype(BF)
    for k, out in enumerate(outs):
        start = pl.multiple_of((where[0] ^ k) * 64, 64)
        out[...] = stream[pl.ds(start, out.shape[0]), :]


def raise_frames(where, before, latent, after, conv, bend, up):
    rows, depth = latent.shape[0] + 16, conv.shape[1]
    width = up.shape[1] * up.shape[2]
    shape = jax.ShapeDtypeStruct((FRAMES, width // 2), BF)
    return plain(
        raise_kernel,
        [shape] * 4,
        [where, before, latent, after, conv, bend[None], up],
        "raise",
        vmem=60,
        flops=6 * 10**9,
        spaces={0: "smem", 4: "any", 6: "any"},
        scratch=[
            pltpu.VMEM((rows + 8, 2 * latent.shape[1]), F32),
            pltpu.VMEM((rows, 8 * latent.shape[1]), BF),
            pltpu.VMEM(conv.shape, BF),
            pltpu.VMEM(up.shape, BF),
            pltpu.VMEM((depth, width), BF),
            pltpu.VMEM((rows, depth), BF),
            pltpu.VMEM((rows + 8, width), F32),
            pltpu.VMEM((rows, width // 2), BF),
            pltpu.SemaphoreType.DMA((9,)),
        ],
    )


def units_kernel(taps, where_ref, parts, w_scr, slopes, outs, *scr):
    stream, held, wides = scr[0], scr[1], scr[2:4]
    me, first = where_ref[0], where_ref[1]
    depth = 512
    frames = parts[0].shape[0]

    held[...] = jnp.zeros_like(held)
    for t in range(4):

        @pl.when(me == t)
        def _(t=t):
            for k in range(4):
                cols = slice((t ^ k) * 128, ((t ^ k) + 1) * 128)
                for j in range(8):
                    piece = parts[k][:, j * 128 : (j + 1) * 128]
                    stream[j * frames : (j + 1) * frames, cols] = piece.astype(F32)

    row = lax.broadcasted_iota(jnp.int32, (frames, depth), 0)
    for u in range(3):
        spread = 3**u
        per_turn, inverse = turns(slopes[2 * u : 2 * u + 1, :])
        for j in range(8):
            step = first + j + 8 * row
            inside = (step >= 0) & (step < 65536)
            entering = snake(stream[j * frames : (j + 1) * frames, :], per_turn, inverse)
            held[j, 8 : 8 + frames, :] = jnp.where(inside, entering, 0.0)
        per_turn, inverse = turns(slopes[2 * u + 1 : 2 * u + 2, :])
        for half, wide in enumerate(wides):
            for m in range(-3 * spread, 8 + 3 * spread):
                spots = []
                for k in range(taps):
                    j = m - (k - 3) * spread - 4 * half
                    if 0 <= j < 4:
                        spots.append((j, k))
                if spots:
                    start = 8 + m // 8
                    moved = held[m % 8, start : start + frames, :].astype(BF)
                    for j, k in spots:
                        wide[j * frames : (j + 1) * frames, k * depth : (k + 1) * depth] = moved
            widened = jnp.dot(
                wide[...], w_scr[u, :taps].reshape(taps * depth, depth), preferred_element_type=F32
            )
            inner = snake(widened, per_turn, inverse).astype(BF)
            rows = slice(half * 4 * frames, (half + 1) * 4 * frames)
            stream[rows, :] += jnp.dot(
                inner, w_scr[u, taps], preferred_element_type=F32
            )
    for t in range(4):

        @pl.when(me == t)
        def _(t=t):
            for k in range(4):
                cols = slice((t ^ k) * 128, ((t ^ k) + 1) * 128)
                for j in range(8):
                    start = j * frames + REACH
                    piece = stream[start : start + 64, cols]
                    outs[k][:, j * 128 : (j + 1) * 128] = piece.astype(BF)


def assemble_kernel(taps, where, *refs):
    parts, (out, slopes, bends, sems, bend_sems) = refs[:4], refs[4:]
    depth = out.shape[2]

    def move(u, k):
        cols = pl.ds(pl.multiple_of((where[0] ^ k) * 128, 128), 128)
        return pltpu.make_async_copy(
            parts[k].at[pl.ds(u * (taps + 1), taps + 1)],
            out.at[u, pl.ds(0, taps + 1), :, cols],
            sems.at[u, k],
        )

    def bend_move(k):
        return pltpu.make_async_copy(
            parts[k].at[3 * (taps + 1), pl.ds(0, 32)], bends.at[k], bend_sems.at[k]
        )

    for k in range(4):
        bend_move(k).start()
    for u in range(3):
        for k in range(4):
            move(u, k).start()
    for k in range(4):
        bend_move(k).wait()
    for t in range(4):

        @pl.when(where[0] == t)
        def _(t=t):
            for k in range(4):
                cols = slice((t ^ k) * 128, ((t ^ k) + 1) * 128)
                bend = bends[k].astype(F32)
                slopes[:, cols] = bend[:8] + bend[8:16] + bend[16:24]

    for u in range(3):
        for k in range(4):
            move(u, k).wait()


def assemble(where, weights, taps):
    depth = weights[0].shape[1]
    shapes = [
        jax.ShapeDtypeStruct((3, taps + 1, depth, depth), BF),
        jax.ShapeDtypeStruct((8, depth), F32),
    ]
    spaces = {0: "smem", 1: "any", 2: "any", 3: "any", 4: "any"}
    return plain(
        functools.partial(assemble_kernel, taps),
        shapes,
        [where, *weights],
        "assemble",
        vmem=16,
        flops=6 * 10**9,
        spaces=spaces,
        scratch=[
            pltpu.VMEM((4, 32, 128), BF),
            pltpu.SemaphoreType.DMA((3, 4)),
            pltpu.SemaphoreType.DMA((4,)),
        ],
    )


def units(where, parts, whole, slopes):
    frames = parts[0].shape[0]
    taps, depth = whole.shape[1] - 1, whole.shape[2]

    def body(where_ref, p0, p1, p2, p3, w, s, o0, o1, o2, o3, *scr):
        units_kernel(taps, where_ref, (p0, p1, p2, p3), w, s, (o0, o1, o2, o3), *scr)

    return plain(
        body,
        [jax.ShapeDtypeStruct((64, 1024), BF)] * 4,
        [where, *parts, whole, slopes],
        "units",
        vmem=30,
        flops=12 * 10**9,
        spaces={0: "smem"},
        scratch=[
            pltpu.VMEM((8 * frames, depth), F32),
            pltpu.VMEM((8, frames + 16, depth), F32),
            pltpu.VMEM((4 * frames, taps * depth), BF),
            pltpu.VMEM((4 * frames, taps * depth), BF),
        ],
    )


def place_kernel(where, p0, p1, p2, p3, out):
    frames = p0.shape[0]
    for t in range(4):

        @pl.when(where[0] == t)
        def _(t=t):
            for k, part in enumerate((p0, p1, p2, p3)):
                for j in range(8):
                    rows = pl.ds((t ^ k) * 8 * frames + j, frames, stride=8)
                    out[rows, :] = part[:, j * 128 : (j + 1) * 128].astype(F32)


def pack(dilated, point, bend, after):
    def body(x, y, z, _, out, token, scr, sems):
        token[...] = jnp.zeros_like(token)
        units, taps, depth = x.shape[:3]
        moves = []
        for u in range(units):
            at = u * (taps + 1)
            moves.append((x.at[u], pl.ds(at, taps)))
            moves.append((y.at[pl.ds(u, 1)], pl.ds(at + taps, 1)))
        for i, (source, place) in enumerate(moves):
            pltpu.make_async_copy(source, scr.at[place], sems.at[0, i]).start()
        tail = scr.shape[0] - 1
        scr[tail] = jnp.zeros(scr.shape[1:], BF)
        scr[tail, :24, :] = z[...]
        pltpu.make_async_copy(scr.at[tail], out.at[tail], sems.at[1, len(moves)]).start()
        for i, (source, place) in enumerate(moves):
            pltpu.make_async_copy(source, scr.at[place], sems.at[0, i]).wait()
            pltpu.make_async_copy(scr.at[place], out.at[place], sems.at[1, i]).start()
        for i, (source, place) in enumerate(moves):
            pltpu.make_async_copy(scr.at[place], out.at[place], sems.at[1, i]).wait()
        pltpu.make_async_copy(scr.at[tail], out.at[tail], sems.at[1, len(moves)]).wait()

    anywhere = pl.BlockSpec(memory_space=pl.ANY)
    units, taps, depth, width = dilated.shape
    shape = (units * (taps + 1) + 1, depth, width)
    return pl.pallas_call(
        body,
        out_shape=[jax.ShapeDtypeStruct(shape, BF), TOKEN],
        in_specs=[anywhere] * 2 + [pl.BlockSpec(memory_space=pltpu.VMEM), anywhere],
        out_specs=[anywhere, pl.BlockSpec(memory_space=pltpu.VMEM)],
        scratch_shapes=[pltpu.VMEM(shape, BF), pltpu.SemaphoreType.DMA((2, 7))],
        cost_estimate=pl.CostEstimate(flops=0, bytes_accessed=2**23, transcendentals=0),
        compiler_params=pltpu.CompilerParams(vmem_limit_bytes=60 * MIB),
        name="pack",
    )(dilated, point, bend, after)


def tie(x, *after):
    anywhere = pl.BlockSpec(memory_space=pl.ANY)
    return pl.pallas_call(
        lambda *refs: None,
        out_shape=jax.ShapeDtypeStruct(x.shape, x.dtype),
        in_specs=[anywhere] * (1 + len(after)),
        out_specs=anywhere,
        input_output_aliases={0: 0},
        name="tie",
    )(x, *after)


def local(
    queries,
    key_rows,
    value_rows,
    residual,
    branch_gate,
    out_weight,
    final_scale,
    final_shift,
    final_weight,
    input_conv,
    lift_slopes,
    up_weight,
    unit_slopes,
    unit_dilated,
    unit_point,
):
    frames = queries.shape[0]
    seq, tp = lax.axis_index("seq"), lax.axis_index("tp")
    low = seq < 16
    share = 2 * frames
    begin = seq * frames - (EXTRA - 3)
    where = [tp, seq * 8 * frames + tp * share - 8 * REACH, seq // 16, begin, (seq // 4) % 4]
    where = jnp.stack(where)
    where = where.astype(jnp.int32)

    def along_x(d):
        return [(i, (i & ~3) | ((i + d) & 3)) for i in range(32)]

    def along_y(d):
        return [(i, (i & ~12) | ((i + 4 * d) & 12)) for i in range(32)]

    def across(k):
        return [(i, i ^ k) for i in range(4)]

    def column(z, k):
        return [(4 * i + j, 4 * (i ^ (16 * z)) + (j ^ k)) for i in range(32) for j in range(4)]

    def send_column(x, z, k):
        return lax.ppermute(x, ("seq", "tp"), column(z, k))

    shape = jax.ShapeDtypeStruct((9 * HD, frames), BF)
    mine, theirs = plain(
        split_kernel,
        [shape, shape],
        [where, queries, key_rows, value_rows],
        "split",
        vmem=60,
        spaces={0: "smem", 1: "any", 2: "any", 3: "any"},
        scratch=[pltpu.VMEM((3,) + queries.shape, BF), pltpu.SemaphoreType.DMA((3,))],
    )
    theirs = send_column(theirs, 1, 0)
    taps = unit_dilated.shape[1]
    bend = jnp.concatenate(
        [jnp.pad(p, ((0, 2), (0, 0))) for p in three_parts(unit_slopes.reshape(6, 128))]
    )
    packed, token = pack(unit_dilated, unit_point, bend, mine)
    kv_own, token = plain(
        join_kernel,
        [jax.ShapeDtypeStruct((6 * HD, 2 * frames), BF), TOKEN],
        [mine, theirs, token],
        "join",
        spaces={2: "any"},
    )
    q_shape = jax.ShapeDtypeStruct((3 * HD, 2 * frames), BF)
    q_own, q_again, kv_again = plain(
        first_kernel, [q_shape, q_shape, kv_own], [kv_own, mine, theirs], "first"
    )
    order = (1, 3, 2)
    kv_far = [lax.ppermute(kv_own, "seq", along_x(d)) for d in order[:2]]
    q_far = [lax.ppermute(q_own, "seq", along_y(d)) for d in order[:2]]
    q_far.append(lax.ppermute(tie(q_again, q_far[0]), "seq", along_y(2)))
    kv_far.append(lax.ppermute(tie(kv_again, q_far[1]), "seq", along_x(2)))

    out_beyond = send_column(out_weight, 1, 2)
    ready = [prepare(kv) for kv in [kv_own] + kv_far]
    packed = tie(packed, out_beyond, ready[1][2], ready[2][2], *q_far)
    packed_beyond = send_column(packed, 1, 2)
    carries = attend(q_far[:2], ready[:3], last=False)
    out_parts = [
        out_weight,
        lax.ppermute(out_weight, "tp", across(1)),
        out_beyond,
        lax.ppermute(out_beyond, "tp", across(1)),
    ]
    out1, out3 = attend(q_far[:2], ready[3:], carries)
    (out2,) = attend(q_far[2:], ready, after=[out1])
    after = [out2, out_parts[1], out_parts[3]]
    (out0,) = attend([q_own], ready, after=after)
    back = [lax.ppermute(o, "seq", along_y(-d)) for o, d in zip((out1, out3, out2), order)]
    mine, theirs = merge([out0] + back)
    far = send_column(theirs, 1, 0)
    (attended,) = plain(
        rows_kernel,
        [jax.ShapeDtypeStruct((frames, 6 * HD), BF)],
        [where, mine, far],
        "rows",
        spaces={0: "smem"},
    )
    attended = lax.all_gather(attended, "tp")
    latent = project(
        where, attended, out_parts, residual, branch_gate, final_scale, final_shift, final_weight
    )

    up = [(i, i + 1) for i in range(31)]
    down = [(i + 1, i) for i in range(31)]
    before = lax.ppermute(latent[-EXTRA:], "seq", up)
    after = lax.ppermute(latent[:EXTRA], "seq", down)
    conv = input_conv.reshape(-1, input_conv.shape[2])
    parts = raise_frames(where, before, latent, after, conv, lift_slopes, up_weight)
    packed_beyond = tie(packed_beyond, parts[0])
    packed_parts = [packed, lax.ppermute(packed, "tp", across(1)), packed_beyond]
    packed_parts.append(lax.ppermute(packed_beyond, "tp", across(1)))

    parts = [parts[0]] + [lax.ppermute(parts[k], "tp", across(k)) for k in (1, 2, 3)]
    done = units(where, parts, *assemble(where, packed_parts, taps))
    done = [done[0]] + [lax.ppermute(done[k], "tp", across(k)) for k in (1, 2, 3)]
    (decoded,) = plain(
        place_kernel,
        [jax.ShapeDtypeStruct((8 * frames, 128), F32)],
        [where, *done],
        "place",
        spaces={0: "smem"},
    )
    return (latent, decoded)


def solution(mesh):
    placed = (
        P("seq", "tp"),
        P("seq", "tp"),
        P("seq", "tp"),
        P("seq", None),
        P(),
        P("tp", None),
        P(),
        P(),
        P(),
        P(),
        P(),
        P(None, None, "tp"),
        P(None, None, "tp"),
        P(None, None, None, "tp"),
        P(None, None, "tp"),
    )
    return jax.shard_map(
        local,
        mesh=mesh,
        in_specs=placed,
        out_specs=(P("seq", None), P("seq", "tp")),
        check_vma=False,
    )
```

```python
import functools
import math

import jax
import jax.numpy as jnp
from jax import lax
from jax.experimental import pallas as pl
from jax.experimental.pallas import tpu as pltpu
from jax.sharding import PartitionSpec as P

HD = 64
LOG2E = 1.4426950408889634
SINE = (9.869524955749512, -32.46514129638672, 42.64342498779297, -29.426273345947266, 10.581296920776367)
BF = jnp.bfloat16
F32 = jnp.float32
REACH = 5
FRAMES = 80
EXTRA = REACH + 4
MIB = 2**20
TOKEN = jax.ShapeDtypeStruct((8, 128), F32)


def turns(slopes):
    return slopes * (1.0 / math.pi), 1.0 / slopes


def snake(signal, per_turn, inverse):
    part = signal * per_turn
    part = part - jnp.round(part)
    z = part * part
    poly = SINE[4]
    for c in SINE[3::-1]:
        poly = poly * z + c
    return signal + poly * z * inverse


def three_parts(x):
    high = lax.reduce_precision(x, 8, 7)
    mid = lax.reduce_precision(x - high, 8, 7)
    low = x - high - mid
    return high.astype(BF), mid.astype(BF), low.astype(BF)


HEADS = 3
CARRY = HD + 8


def plain(body, shapes, inputs, name, vmem=12, scratch=(), flops=0, spaces=None):
    space = {"smem": pltpu.SMEM, "any": pl.ANY}
    specs = [
        pl.BlockSpec(memory_space=space.get((spaces or {}).get(i), pltpu.VMEM))
        for i in range(len(inputs))
    ]
    return pl.pallas_call(
        body,
        out_shape=[jax.ShapeDtypeStruct(s.shape, s.dtype) for s in shapes],
        in_specs=specs,
        out_specs=[pl.BlockSpec(memory_space=pltpu.VMEM)] * len(shapes),
        scratch_shapes=list(scratch),
        cost_estimate=pl.CostEstimate(flops=flops // 16, bytes_accessed=2**16, transcendentals=0),
        compiler_params=pltpu.CompilerParams(vmem_limit_bytes=vmem * MIB),
        name=name,
    )(*inputs)


def split_kernel(where, q, k, v, mine, theirs, scr, sems):
    width = HEADS * HD
    copies = [pltpu.make_async_copy(r, scr.at[n], sems.at[n]) for n, r in enumerate((q, k, v))]
    for copy in copies:
        copy.start()
    for n, copy in enumerate(copies):
        copy.wait()
        turned = scr[n].astype(F32).T.astype(BF)
        rows = slice(n * width, (n + 1) * width)
        for z in range(2):

            @pl.when(where[2] == z)
            def _(z=z, rows=rows, turned=turned):
                mine[rows, :] = turned[z * width : (z + 1) * width]
                theirs[rows, :] = turned[(1 - z) * width : (2 - z) * width]


def join_kernel(mine, theirs, _, out, token):
    token[...] = jnp.zeros_like(token)
    half = mine.shape[1]
    out[:, :half] = mine[HEADS * HD :, :]
    out[:, half:] = theirs[HEADS * HD :, :]


def first_kernel(kv, mine, theirs, q_out, q_again, kv_again):
    kv_again[...] = kv[...]
    half = mine.shape[1]
    for out in (q_out, q_again):
        out[:, :half] = mine[: HEADS * HD, :]
        out[:, half:] = theirs[: HEADS * HD, :]


def prepare_kernel(kv, k_out, v_out):
    piece = kv.shape[1]
    width = HEADS * HD
    for h in range(HEADS):
        key_part = kv[h * HD : (h + 1) * HD, :]
        k_out[h, :HD, :] = key_part
        k_out[h, HD:, :] = key_part
    values = kv[width:, :].astype(F32)
    first = values[: 2 * HD].T
    last = jnp.concatenate([values[2 * HD :], jnp.zeros((HD, piece), F32)], axis=0).T
    lane = lax.broadcasted_iota(jnp.int32, (piece, 2 * HD), 1)
    ones = jnp.where(lane == HD, 1.0, 0.0)
    v_out[0] = jnp.where(lane < HD, first, ones).astype(BF)
    v_out[1] = jnp.where(lane >= HD, first, jnp.where(lane == 0, 1.0, 0.0)).astype(BF)
    v_out[2] = jnp.where(lane < HD, last, ones).astype(BF)


def prepared(kv):
    piece = kv.shape[1]
    return [
        jax.ShapeDtypeStruct((HEADS, 2 * HD, piece), BF),
        jax.ShapeDtypeStruct((HEADS, piece, 2 * HD), BF),
    ]


def prepare(kv):
    def body(kv, k_out, v_out, token):
        token[...] = jnp.zeros_like(token)
        prepare_kernel(kv, k_out, v_out)

    return plain(body, prepared(kv) + [TOKEN], [kv], "prepare", flops=10**9)


def attend_kernel(q_refs, k_refs, v_refs, c_refs, out_refs, last):
    rows = 256
    row_id = lax.broadcasted_iota(jnp.int32, (16, rows), 0)
    items = [
        (n, block, h)
        for n, q in enumerate(q_refs)
        for block in range(q.shape[1] // rows)
        for h in range(HEADS)
    ]

    def score(n, block, h):
        cols = slice(block * rows, (block + 1) * rows)
        query = q_refs[n][h * HD : (h + 1) * HD, cols].astype(F32) * (LOG2E / math.sqrt(HD))
        high = query.astype(BF).astype(F32)
        both = jnp.concatenate([high, query - high], axis=0).T.astype(BF)
        return [jnp.dot(both, k[h], preferred_element_type=F32) for k in k_refs]

    def finish(n, block, h, scores, stats):
        cols = slice(block * rows, (block + 1) * rows)
        top = functools.reduce(jnp.maximum, scores)
        top = jnp.max(top, axis=1, keepdims=True)
        total = None
        for s, v in zip(scores, v_refs):
            weights = jnp.exp2(s - top).astype(BF)
            part = jnp.dot(weights, v[h], preferred_element_type=F32)
            total = part if total is None else total + part
        lanes = lax.broadcasted_iota(jnp.int32, (rows, 2 * HD), 1)
        spare = 0 if h == 1 else HD
        total = jnp.where(lanes == spare + 1, top, total).T
        sums = total[HD - spare : 2 * HD - spare]
        weight_sum, top = total[spare : spare + 1], total[spare + 1 : spare + 2]
        if not last:
            out_refs[n][h * CARRY : h * CARRY + HD, cols] = sums
            out_refs[n][h * CARRY + HD : (h + 1) * CARRY, cols] = jnp.where(
                row_id[:8] == 0, weight_sum, top
            )
            return stats
        if c_refs:
            at = h * CARRY
            older_sum = c_refs[n][at + HD : at + HD + 1, cols]
            older = c_refs[n][at + HD + 1 : at + HD + 2, cols]
            newer, top = top, jnp.maximum(top, older)
            here, there = jnp.exp2(newer - top), jnp.exp2(older - top)
            sums = sums * here + c_refs[n][at : at + HD, cols] * there
            weight_sum = weight_sum * here + older_sum * there
        level = top + jnp.log2(weight_sum)
        out_refs[n][h * HD : (h + 1) * HD, cols] = (sums / weight_sum).astype(BF)
        first = level.astype(BF).astype(F32)
        second = (level - first).astype(BF).astype(F32)
        third = level - first - second
        for k, part in enumerate((first, second, third)):
            stats = jnp.where(row_id == 3 * h + k, part, stats)
        if h == HEADS - 1:
            out_refs[n][HEADS * HD :, cols] = stats.astype(BF)
            stats = jnp.zeros_like(stats)
        return stats

    stats = jnp.zeros((16, rows), F32)
    ahead = score(*items[0])
    for i, item in enumerate(items):
        scores = ahead
        if i + 1 < len(items):
            ahead = score(*items[i + 1])
        stats = finish(*item, scores, stats)


def attend(q_parts, ready, carries=(), last=True, after=()):
    n, m, c = len(q_parts), len(ready), len(carries)

    def body(*refs):
        ends = (n, n + m, n + 2 * m, n + 2 * m + c)
        groups = [refs[a:b] for a, b in zip((0,) + ends[:-1], ends)]
        attend_kernel(*groups, refs[ends[-1] + len(after) :], last)

    inputs = list(q_parts) + [r[0] for r in ready] + [r[1] for r in ready] + list(carries)
    rows, kind = (HEADS * HD + 16, BF) if last else (HEADS * CARRY, F32)
    return plain(
        body,
        [jax.ShapeDtypeStruct((rows, q.shape[1]), kind) for q in q_parts],
        inputs + list(after),
        "attend",
        vmem=18,
        flops=int(1.5e9) * n * m,
        spaces={len(inputs) + i: "any" for i in range(len(after))},
    )


def merge_kernel(p0, p1, p2, p3, mine, theirs):
    parts = [p[...].astype(F32) for p in (p0, p1, p2, p3)]
    half = mine.shape[1]
    for h in range(HEADS):
        levels = []
        for p in parts:
            r = HEADS * HD + 3 * h
            levels.append(p[r : r + 1] + p[r + 1 : r + 2] + p[r + 2 : r + 3])
        top = functools.reduce(jnp.maximum, levels)
        shares = [jnp.exp2(level - top) for level in levels]
        whole = functools.reduce(jnp.add, shares)
        rows = slice(h * HD, (h + 1) * HD)
        total = functools.reduce(jnp.add, [p[rows] * (s / whole) for p, s in zip(parts, shares)])
        mine[rows, :] = total[:, :half].astype(BF)
        theirs[rows, :] = total[:, half:].astype(BF)


def merge(parts):
    shape = jax.ShapeDtypeStruct((HEADS * HD, parts[0].shape[1] // 2), BF)
    return plain(merge_kernel, [shape, shape], parts, "merge", flops=10**9)


def rows_kernel(where, mine, far, out):
    near_z = where[2]
    for z in range(2):

        @pl.when(near_z == z)
        def _(z=z):
            pair = (far, mine) if z else (mine, far)
            both = jnp.concatenate([p[...].astype(F32) for p in pair], axis=0)
            out[...] = both.T.astype(BF)


def project_kernel(
    where, attended, w0, w1, w2, w3, residual, gate, scale, shift, final, out, scr, held, sems
):
    copies = [
        pltpu.make_async_copy(w, scr.at[k], sems.at[k]) for k, w in enumerate((w0, w1, w2, w3))
    ]
    copies.append(pltpu.make_async_copy(residual, held, sems.at[4]))
    for copy in copies:
        copy.start()
    total = None
    for k in range(4):
        copies[k].wait()
        part = jnp.dot(attended[where[0] ^ k], scr[k], preferred_element_type=F32)
        total = part if total is None else total + part
    copies[4].wait()
    mixed = held[...].astype(F32) + gate[...] * total
    mean = jnp.mean(mixed, axis=1, keepdims=True)
    centred = mixed - mean
    variance = jnp.mean(centred * centred, axis=1, keepdims=True)
    normed = (centred * lax.rsqrt(variance + 1e-06) * scale[...] + shift[...]).astype(BF)
    out[...] = jnp.dot(normed, final[...], preferred_element_type=F32).astype(BF)


def project(where, attended, weights, residual, gate, scale, shift, final):
    shape = jax.ShapeDtypeStruct((residual.shape[0], final.shape[1]), BF)
    inputs = [where, attended, *weights, residual, gate[None], scale[None], shift[None], final]
    return plain(
        project_kernel,
        [shape],
        inputs,
        "project",
        vmem=60,
        flops=4 * 10**9,
        spaces={0: "smem", **{i: "any" for i in range(2, 7)}},
        scratch=[
            pltpu.VMEM((4,) + weights[0].shape, BF),
            pltpu.VMEM(residual.shape, BF),
            pltpu.SemaphoreType.DMA((5,)),
        ],
    )[0]


def raise_kernel(where, before, latent, after, conv, bend, up, *refs):
    outs = refs[:4]
    wide, columns, conv_scr, raw, up_scr, lifted, taps, stream, sems = refs[4:]
    depth_up, count, channels = up.shape
    parts = 8
    block = depth_up // parts
    places = [pl.ds(i * block, block) for i in range(parts)]
    ins = [pltpu.make_async_copy(up.at[p], raw.at[p], sems.at[i]) for i, p in enumerate(places)]
    conv_in = pltpu.make_async_copy(conv, conv_scr, sems.at[parts])
    conv_in.start()
    for copy in ins:
        copy.start()
    size = count * count
    to = lax.broadcasted_iota(jnp.int32, (size, size), 0)
    of = lax.broadcasted_iota(jnp.int32, (size, size), 1)
    swap = jnp.where(of == (to % count) * count + to // count, 1.0, 0.0).astype(BF)

    def turn(i):
        ins[i].wait()
        for c in range(i * block, (i + 1) * block, 2 * count):
            pair = [
                raw[c + n * count : c + (n + 1) * count].reshape(size, channels) for n in range(2)
            ]
            pair = jnp.concatenate(pair, axis=1)
            moved = jnp.dot(swap, pair, preferred_element_type=F32).astype(BF)
            for n in range(2):
                for j in range(count):
                    up_scr[
                        c + n * count : c + (n + 1) * count, j * channels : (j + 1) * channels
                    ] = moved[j * count : (j + 1) * count, n * channels : (n + 1) * channels]

    rows = columns.shape[0]
    frames, width = latent.shape
    wide[...] = jnp.zeros_like(wide)
    wide[:EXTRA, :width] = before[...].astype(F32)
    wide[EXTRA : EXTRA + frames, :width] = latent[...].astype(F32)
    wide[EXTRA + frames : 2 * EXTRA + frames, :width] = after[...].astype(F32)
    for k in range(0, 8, 2):
        pair = wide[k : k + rows, :]
        if k < 6:
            pair = pair + pltpu.roll(wide[k + 1 : k + 1 + rows, :], width, 1)
        columns[:, k * width : (k + 2) * width] = pair.astype(BF)
    step = 512
    frame = where[3] + lax.broadcasted_iota(jnp.int32, (rows, step), 0)
    inside = (frame >= 0) & (frame < 8192)
    conv_in.wait()
    depth = conv.shape[0]
    for c in range(0, lifted.shape[1], step):
        cols = slice(c, c + step)
        opened = jnp.dot(columns[:, :depth], conv_scr[:, cols], preferred_element_type=F32)
        up_part = snake(opened, *turns(bend[:, cols]))
        lifted[:, cols] = jnp.where(inside, up_part, 0.0).astype(BF)
        turn(c // step * 2)
        turn(c // step * 2 + 1)
    taps[rows:, :] = jnp.zeros((taps.shape[0] - rows, taps.shape[1]), F32)
    for c in range(0, taps.shape[1], step):
        cols = slice(c, c + step)
        taps[:rows, cols] = jnp.dot(lifted[...], up_scr[:, cols], preferred_element_type=F32)
    before_part = taps[0:rows, 3 * step :]
    after_part = taps[2 : 2 + rows, :step]
    stream[:, :step] = (taps[1 : 1 + rows, step : 2 * step] + before_part).astype(BF)
    stream[:, step:] = (taps[1 : 1 + rows, 2 * step : 3 * step] + after_part).astype(BF)
    for k, out in enumerate(outs):
        start = pl.multiple_of((where[0] ^ k) * 64, 64)
        out[...] = stream[pl.ds(start, out.shape[0]), :]


def raise_frames(where, before, latent, after, conv, bend, up):
    rows, depth = latent.shape[0] + 16, conv.shape[1]
    width = up.shape[1] * up.shape[2]
    shape = jax.ShapeDtypeStruct((FRAMES, width // 2), BF)
    return plain(
        raise_kernel,
        [shape] * 4,
        [where, before, latent, after, conv, bend[None], up],
        "raise",
        vmem=60,
        flops=6 * 10**9,
        spaces={0: "smem", 4: "any", 6: "any"},
        scratch=[
            pltpu.VMEM((rows + 8, 2 * latent.shape[1]), F32),
            pltpu.VMEM((rows, 8 * latent.shape[1]), BF),
            pltpu.VMEM(conv.shape, BF),
            pltpu.VMEM(up.shape, BF),
            pltpu.VMEM((depth, width), BF),
            pltpu.VMEM((rows, depth), BF),
            pltpu.VMEM((rows + 8, width), F32),
            pltpu.VMEM((rows, width // 2), BF),
            pltpu.SemaphoreType.DMA((9,)),
        ],
    )


def units_kernel(taps, where_ref, parts, w_scr, slopes, outs, *scr):
    stream, held, wides = scr[0], scr[1], scr[2:4]
    me, first = where_ref[0], where_ref[1]
    depth = 512
    frames = parts[0].shape[0]

    held[...] = jnp.zeros_like(held)
    for t in range(4):

        @pl.when(me == t)
        def _(t=t):
            for k in range(4):
                cols = slice((t ^ k) * 128, ((t ^ k) + 1) * 128)
                for j in range(8):
                    piece = parts[k][:, j * 128 : (j + 1) * 128]
                    stream[j * frames : (j + 1) * frames, cols] = piece.astype(F32)

    row = lax.broadcasted_iota(jnp.int32, (frames, depth), 0)
    for u in range(3):
        spread = 3**u
        per_turn, inverse = turns(slopes[2 * u : 2 * u + 1, :])
        for j in range(8):
            step = first + j + 8 * row
            inside = (step >= 0) & (step < 65536)
            entering = snake(stream[j * frames : (j + 1) * frames, :], per_turn, inverse)
            held[j, 8 : 8 + frames, :] = jnp.where(inside, entering, 0.0)
        per_turn, inverse = turns(slopes[2 * u + 1 : 2 * u + 2, :])
        both = []
        for half, wide in enumerate(wides):
            for m in range(-3 * spread, 8 + 3 * spread):
                spots = []
                for k in range(taps):
                    j = m - (k - 3) * spread - 4 * half
                    if 0 <= j < 4:
                        spots.append((j, k))
                if spots:
                    start = 8 + m // 8
                    moved = held[m % 8, start : start + frames, :].astype(BF)
                    for j, k in spots:
                        wide[j * frames : (j + 1) * frames, k * depth : (k + 1) * depth] = moved
            widened = jnp.dot(
                wide[...], w_scr[u, :taps].reshape(taps * depth, depth), preferred_element_type=F32
            )
            both.append(widened)
        for half, widened in enumerate(both):
            inner = snake(widened, per_turn, inverse).astype(BF)
            rows = slice(half * 4 * frames, (half + 1) * 4 * frames)
            stream[rows, :] += jnp.dot(
                inner, w_scr[u, taps], preferred_element_type=F32
            )
    for t in range(4):

        @pl.when(me == t)
        def _(t=t):
            for k in range(4):
                cols = slice((t ^ k) * 128, ((t ^ k) + 1) * 128)
                for j in range(8):
                    start = j * frames + REACH
                    piece = stream[start : start + 64, cols]
                    outs[k][:, j * 128 : (j + 1) * 128] = piece.astype(BF)


def assemble_kernel(taps, where, *refs):
    parts, (out, slopes, bends, sems, bend_sems) = refs[:4], refs[4:]
    depth = out.shape[2]

    def move(u, k):
        cols = pl.ds(pl.multiple_of((where[0] ^ k) * 128, 128), 128)
        return pltpu.make_async_copy(
            parts[k].at[pl.ds(u * (taps + 1), taps + 1)],
            out.at[u, pl.ds(0, taps + 1), :, cols],
            sems.at[u, k],
        )

    def bend_move(k):
        return pltpu.make_async_copy(
            parts[k].at[3 * (taps + 1), pl.ds(0, 32)], bends.at[k], bend_sems.at[k]
        )

    for k in range(4):
        bend_move(k).start()
    for u in range(3):
        for k in range(4):
            move(u, k).start()
    for k in range(4):
        bend_move(k).wait()
    for t in range(4):

        @pl.when(where[0] == t)
        def _(t=t):
            for k in range(4):
                cols = slice((t ^ k) * 128, ((t ^ k) + 1) * 128)
                bend = bends[k].astype(F32)
                slopes[:, cols] = bend[:8] + bend[8:16] + bend[16:24]

    for u in range(3):
        for k in range(4):
            move(u, k).wait()


def assemble(where, weights, taps):
    depth = weights[0].shape[1]
    shapes = [
        jax.ShapeDtypeStruct((3, taps + 1, depth, depth), BF),
        jax.ShapeDtypeStruct((8, depth), F32),
    ]
    spaces = {0: "smem", 1: "any", 2: "any", 3: "any", 4: "any"}
    return plain(
        functools.partial(assemble_kernel, taps),
        shapes,
        [where, *weights],
        "assemble",
        vmem=16,
        flops=6 * 10**9,
        spaces=spaces,
        scratch=[
            pltpu.VMEM((4, 32, 128), BF),
            pltpu.SemaphoreType.DMA((3, 4)),
            pltpu.SemaphoreType.DMA((4,)),
        ],
    )


def units(where, parts, whole, slopes):
    frames = parts[0].shape[0]
    taps, depth = whole.shape[1] - 1, whole.shape[2]

    def body(where_ref, p0, p1, p2, p3, w, s, o0, o1, o2, o3, *scr):
        units_kernel(taps, where_ref, (p0, p1, p2, p3), w, s, (o0, o1, o2, o3), *scr)

    return plain(
        body,
        [jax.ShapeDtypeStruct((64, 1024), BF)] * 4,
        [where, *parts, whole, slopes],
        "units",
        vmem=30,
        flops=12 * 10**9,
        spaces={0: "smem"},
        scratch=[
            pltpu.VMEM((8 * frames, depth), F32),
            pltpu.VMEM((8, frames + 16, depth), F32),
            pltpu.VMEM((4 * frames, taps * depth), BF),
            pltpu.VMEM((4 * frames, taps * depth), BF),
        ],
    )


def place_kernel(where, p0, p1, p2, p3, out):
    frames = p0.shape[0]
    for t in range(4):

        @pl.when(where[0] == t)
        def _(t=t):
            for k, part in enumerate((p0, p1, p2, p3)):
                for j in range(8):
                    rows = pl.ds((t ^ k) * 8 * frames + j, frames, stride=8)
                    out[rows, :] = part[:, j * 128 : (j + 1) * 128].astype(F32)


def pack(dilated, point, bend, after):
    def body(x, y, z, _, out, token, scr, sems):
        token[...] = jnp.zeros_like(token)
        units, taps, depth = x.shape[:3]
        moves = []
        for u in range(units):
            at = u * (taps + 1)
            moves.append((x.at[u], pl.ds(at, taps)))
            moves.append((y.at[pl.ds(u, 1)], pl.ds(at + taps, 1)))
        for i, (source, place) in enumerate(moves):
            pltpu.make_async_copy(source, scr.at[place], sems.at[0, i]).start()
        tail = scr.shape[0] - 1
        scr[tail] = jnp.zeros(scr.shape[1:], BF)
        scr[tail, :24, :] = z[...]
        pltpu.make_async_copy(scr.at[tail], out.at[tail], sems.at[1, len(moves)]).start()
        for i, (source, place) in enumerate(moves):
            pltpu.make_async_copy(source, scr.at[place], sems.at[0, i]).wait()
            pltpu.make_async_copy(scr.at[place], out.at[place], sems.at[1, i]).start()
        for i, (source, place) in enumerate(moves):
            pltpu.make_async_copy(scr.at[place], out.at[place], sems.at[1, i]).wait()
        pltpu.make_async_copy(scr.at[tail], out.at[tail], sems.at[1, len(moves)]).wait()

    anywhere = pl.BlockSpec(memory_space=pl.ANY)
    units, taps, depth, width = dilated.shape
    shape = (units * (taps + 1) + 1, depth, width)
    return pl.pallas_call(
        body,
        out_shape=[jax.ShapeDtypeStruct(shape, BF), TOKEN],
        in_specs=[anywhere] * 2 + [pl.BlockSpec(memory_space=pltpu.VMEM), anywhere],
        out_specs=[anywhere, pl.BlockSpec(memory_space=pltpu.VMEM)],
        scratch_shapes=[pltpu.VMEM(shape, BF), pltpu.SemaphoreType.DMA((2, 7))],
        cost_estimate=pl.CostEstimate(flops=0, bytes_accessed=2**23, transcendentals=0),
        compiler_params=pltpu.CompilerParams(vmem_limit_bytes=60 * MIB),
        name="pack",
    )(dilated, point, bend, after)


def tie(x, *after):
    anywhere = pl.BlockSpec(memory_space=pl.ANY)
    return pl.pallas_call(
        lambda *refs: None,
        out_shape=jax.ShapeDtypeStruct(x.shape, x.dtype),
        in_specs=[anywhere] * (1 + len(after)),
        out_specs=anywhere,
        input_output_aliases={0: 0},
        name="tie",
    )(x, *after)


def local(
    queries,
    key_rows,
    value_rows,
    residual,
    branch_gate,
    out_weight,
    final_scale,
    final_shift,
    final_weight,
    input_conv,
    lift_slopes,
    up_weight,
    unit_slopes,
    unit_dilated,
    unit_point,
):
    frames = queries.shape[0]
    seq, tp = lax.axis_index("seq"), lax.axis_index("tp")
    low = seq < 16
    share = 2 * frames
    begin = seq * frames - (EXTRA - 3)
    where = [tp, seq * 8 * frames + tp * share - 8 * REACH, seq // 16, begin, (seq // 4) % 4]
    where = jnp.stack(where)
    where = where.astype(jnp.int32)

    def along_x(d):
        return [(i, (i & ~3) | ((i + d) & 3)) for i in range(32)]

    def along_y(d):
        return [(i, (i & ~12) | ((i + 4 * d) & 12)) for i in range(32)]

    def across(k):
        return [(i, i ^ k) for i in range(4)]

    def column(z, k):
        return [(4 * i + j, 4 * (i ^ (16 * z)) + (j ^ k)) for i in range(32) for j in range(4)]

    def send_column(x, z, k):
        return lax.ppermute(x, ("seq", "tp"), column(z, k))

    shape = jax.ShapeDtypeStruct((9 * HD, frames), BF)
    mine, theirs = plain(
        split_kernel,
        [shape, shape],
        [where, queries, key_rows, value_rows],
        "split",
        vmem=60,
        spaces={0: "smem", 1: "any", 2: "any", 3: "any"},
        scratch=[pltpu.VMEM((3,) + queries.shape, BF), pltpu.SemaphoreType.DMA((3,))],
    )
    theirs = send_column(theirs, 1, 0)
    taps = unit_dilated.shape[1]
    bend = jnp.concatenate(
        [jnp.pad(p, ((0, 2), (0, 0))) for p in three_parts(unit_slopes.reshape(6, 128))]
    )
    packed, token = pack(unit_dilated, unit_point, bend, mine)
    kv_own, token = plain(
        join_kernel,
        [jax.ShapeDtypeStruct((6 * HD, 2 * frames), BF), TOKEN],
        [mine, theirs, token],
        "join",
        spaces={2: "any"},
    )
    q_shape = jax.ShapeDtypeStruct((3 * HD, 2 * frames), BF)
    q_own, q_again, kv_again = plain(
        first_kernel, [q_shape, q_shape, kv_own], [kv_own, mine, theirs], "first"
    )
    order = (1, 3, 2)
    kv_far = [lax.ppermute(kv_own, "seq", along_x(d)) for d in order[:2]]
    q_far = [lax.ppermute(q_own, "seq", along_y(d)) for d in order[:2]]
    q_far.append(lax.ppermute(tie(q_again, q_far[0]), "seq", along_y(2)))
    kv_far.append(lax.ppermute(tie(kv_again, q_far[1]), "seq", along_x(2)))

    out_beyond = send_column(out_weight, 1, 2)
    ready = [prepare(kv) for kv in [kv_own] + kv_far]
    packed = tie(packed, out_beyond, ready[1][2], ready[2][2], *q_far)
    packed_beyond = send_column(packed, 1, 2)
    carries = attend(q_far[:2], ready[:3], last=False)
    out_parts = [
        out_weight,
        lax.ppermute(out_weight, "tp", across(1)),
        out_beyond,
        lax.ppermute(out_beyond, "tp", across(1)),
    ]
    out1, out3 = attend(q_far[:2], ready[3:], carries)
    (out2,) = attend(q_far[2:], ready, after=[out1])
    after = [out2, out_parts[1], out_parts[3]]
    (out0,) = attend([q_own], ready, after=after)
    back = [lax.ppermute(o, "seq", along_y(-d)) for o, d in zip((out1, out3, out2), order)]
    mine, theirs = merge([out0] + back)
    far = send_column(theirs, 1, 0)
    (attended,) = plain(
        rows_kernel,
        [jax.ShapeDtypeStruct((frames, 6 * HD), BF)],
        [where, mine, far],
        "rows",
        spaces={0: "smem"},
    )
    attended = lax.all_gather(attended, "tp")
    latent = project(
        where, attended, out_parts, residual, branch_gate, final_scale, final_shift, final_weight
    )

    up = [(i, i + 1) for i in range(31)]
    down = [(i + 1, i) for i in range(31)]
    before = lax.ppermute(latent[-EXTRA:], "seq", up)
    after = lax.ppermute(latent[:EXTRA], "seq", down)
    conv = input_conv.reshape(-1, input_conv.shape[2])
    parts = raise_frames(where, before, latent, after, conv, lift_slopes, up_weight)
    packed_beyond = tie(packed_beyond, parts[0])
    packed_parts = [packed, lax.ppermute(packed, "tp", across(1)), packed_beyond]
    packed_parts.append(lax.ppermute(packed_beyond, "tp", across(1)))

    parts = [parts[0]] + [lax.ppermute(parts[k], "tp", across(k)) for k in (1, 2, 3)]
    done = units(where, parts, *assemble(where, packed_parts, taps))
    done = [done[0]] + [lax.ppermute(done[k], "tp", across(k)) for k in (1, 2, 3)]
    (decoded,) = plain(
        place_kernel,
        [jax.ShapeDtypeStruct((8 * frames, 128), F32)],
        [where, *done],
        "place",
        spaces={0: "smem"},
    )
    return (latent, decoded)


def solution(mesh):
    placed = (
        P("seq", "tp"),
        P("seq", "tp"),
        P("seq", "tp"),
        P("seq", None),
        P(),
        P("tp", None),
        P(),
        P(),
        P(),
        P(),
        P(),
        P(None, None, "tp"),
        P(None, None, "tp"),
        P(None, None, None, "tp"),
        P(None, None, "tp"),
    )
    return jax.shard_map(
        local,
        mesh=mesh,
        in_specs=placed,
        out_specs=(P("seq", None), P("seq", "tp")),
        check_vma=False,
    )
```
